32 devices in a mesh: sub: 4 (over z), cgrp: 8 (over y, x, core).
Axes of the slice: x: 2, y: 2, z: 4, core: 2. Of those that a mesh axis runs over, the one named last changes fastest.
Arguments:
- source: float32 [256, 32768], P('sub', 'cgrp'), may hold values from -7.5 to 7.5
- capacity: float32 [256, 32768], P('sub', 'cgrp'), may hold values from 0.01 to 1
- fd_weights: float32 [256, 32768], P('sub', 'cgrp'), may hold values from 0.02 to 1
- fd_modes: float32 [3, 64, 64], replicated, may hold values from -0.75 to 0.75
- face_modes: float32 [2, 128, 64], replicated, may hold values from -0.75 to 0.75
- coarse_map: int32 [4, 8, 6, 128], P('sub', 'cgrp'), may hold values from 0 to 24575, as said below
- fsai_cols: int32 [192, 8], P(('sub', 'cgrp')), may hold values from 0 to 191
- fsai_blocks: float32 [192, 8, 128, 128], P(('sub', 'cgrp')), may hold values from -0.1875 to 0.1875
Outputs:
- solution: float32 [256, 32768], P('sub', 'cgrp')
- residual: float32 [256, 32768], P('sub', 'cgrp')
The draws below stay inside these ranges and needn't reach their ends.
Inputs may be any that keep to these rules, and one draw needn't show every extreme that they name: `coarse_map`: entries are numbered by owner: with d = s * 8 + t, face f of subdomain (s, t) takes the entries (6 d + f) * 128 to (6 d + f) * 128 + 127, each once, in an order of its own; except that face 0 of a subdomain with s > 0 takes exactly the entries of face 1 of subdomain (s - 1, t), and face 2 of a subdomain with t > 0 exactly those of face 3 of subdomain (s, t - 1), function k of both sides taking the same entry.
All inputs are finite; a program needn't handle non-finite values.
Results may differ from the reference program's by a relative error of at most 0.0001.
Values sent between devices are 32-bit elements; how exact they have to be, the bound alone decides.
A program may use at most 64 MiB of HBM per device.

```python
import math
import jax
import jax.numpy as jnp
from jax import lax

C = 64
CF = 128
BS = 128
NNZB = 8
ITERS = 1
SDX = 4
SDY = 8
NX = 256
NY = 512
NZ = 64
NCOARSE = 24576
NBLK = 192


def draw_source(key, part):
    ramp = 1.0 + 2.0 * jnp.arange(NX, dtype=jnp.float32) / (NX - 1)
    field = ramp[:, None, None] * jnp.clip(jax.random.normal(key, (NX, NY, NZ), jnp.float32), -2.5, 2.5)
    return field.reshape(NX, NY * NZ)


def draw_coarse_map(key, part):
    first = jnp.arange(SDX, dtype=jnp.int32)[:, None] * jnp.ones((1, SDY), jnp.int32)
    second = jnp.ones((SDX, 1), jnp.int32) * jnp.arange(SDY, dtype=jnp.int32)[None, :]
    device = first * SDY + second
    inner_first = (first > 0).astype(jnp.int32)
    inner_second = (second > 0).astype(jnp.int32)
    low_first = (device - SDY * inner_first) * 6 + inner_first
    low_second = (device - inner_second) * 6 + 2 + inner_second
    owners = jnp.stack([low_first, device * 6 + 1, low_second, device * 6 + 3, device * 6 + 4, device * 6 + 5], axis=-1)
    scores = jax.random.randint(key, (SDX * SDY * 6, CF), 0, 2 ** 20) * CF
    scores = scores + jnp.arange(CF, dtype=jnp.int32)[None, :]
    order = jnp.argsort(scores, axis=1).astype(jnp.int32)
    return (owners[..., None] * CF + order[owners]).astype(jnp.int32)


def set_ends(result, own_key, smallest, largest):
    longest = result.shape.index(max(result.shape))
    spots = []
    for shift in (0, 1):
        where = [jax.random.randint(jax.random.fold_in(own_key, axis), (), 0, length) for axis, length in enumerate(result.shape)]
        where[longest] = (where[longest] + shift) % result.shape[longest]
        spots.append(tuple(where))
    return result.at[spots[0]].set(smallest).at[spots[1]].set(largest)


def level_of(rng, dims, shards, smallest, high):
    loudness, own = 1.0, jax.random.fold_in(rng, 6)
    for axis_at, shards_of in shards:
        heights = jnp.exp(jax.random.uniform(jax.random.fold_in(own, axis_at), (shards_of,), jnp.float32, smallest / len(shards), high / len(shards)))
        loudness = loudness * jnp.repeat(heights, dims[axis_at] // shards_of).reshape([-1 if axis == axis_at else 1 for axis in range(len(dims))])
    return loudness


def normal_values(rng, dims, scale, limit, pieces=(), kind=jnp.bfloat16):
    array = jax.random.normal(rng, dims, jnp.float32) * scale
    if len(pieces) > 0:
        array = level_of(rng, dims, pieces, -0.22, 0.18) * array
    return jnp.clip(array, min=-limit, max=limit).astype(kind)


def setup_inputs(seed: int = 0) -> dict:
    streams_of = jax.random.split(jax.random.key(seed), 9)
    source = draw_source(jax.random.fold_in(streams_of[8], 71), 0)
    capacity = jnp.clip(jnp.exp(math.log(1.0) - 4.6051702 * jax.random.uniform(streams_of[1], (NX, NY * NZ), jnp.float32) ** level_of(streams_of[1], (NX, NY * NZ), ((0, 4), (1, 8)), -0.2, 0.2)), 0.01, 1.0)
    fd_weights = jnp.clip(jnp.exp(math.log(1.0) - 3.912023 * jax.random.uniform(streams_of[2], (NX, NY * NZ), jnp.float32) ** level_of(streams_of[2], (NX, NY * NZ), ((0, 4), (1, 8)), -0.2, 0.2)), 0.02, 1.0)
    fd_modes = normal_values(streams_of[3], (3, C, C), C ** -0.5, 0.75, (), jnp.float32)
    face_modes = normal_values(streams_of[4], (2, CF, C), (CF // 2) ** -0.5, 0.75, (), jnp.float32)
    coarse_map = draw_coarse_map(jax.random.fold_in(streams_of[8], 71), 0)
    fsai_cols = set_ends(jax.random.randint(streams_of[6], (NBLK, NNZB), 0, NBLK), jax.random.fold_in(streams_of[6], 1), 0, NBLK - 1).astype(jnp.int32)
    fsai_blocks = normal_values(streams_of[7], (NBLK, NNZB, BS, BS), (NNZB * BS) ** -0.5, 0.1875, ((0, 32),), jnp.float32)
    return dict(source=source, capacity=capacity, fd_weights=fd_weights, fd_modes=fd_modes, face_modes=face_modes, coarse_map=coarse_map, fsai_cols=fsai_cols, fsai_blocks=fsai_blocks)


highest = lax.Precision.HIGHEST
along_first = 1.0
along_second = 0.6
along_third = 2.5


def operate(field, capacity):
    padded = jnp.pad(field, 1)
    first = padded[2:, 1:-1, 1:-1] + padded[:-2, 1:-1, 1:-1]
    second = padded[1:-1, 2:, 1:-1] + padded[1:-1, :-2, 1:-1]
    third = padded[1:-1, 1:-1, 2:] + padded[1:-1, 1:-1, :-2]
    diagonal = capacity + 2.0 * (along_first + along_second + along_third)
    return diagonal * field - along_first * first - along_second * second - along_third * third


def to_blocks(field):
    return field.reshape(SDX, C, SDY, C, C).transpose(0, 2, 1, 3, 4)


def from_blocks(blocks):
    return blocks.transpose(0, 2, 1, 3, 4).reshape(NX, NY, NZ)


def transform(blocks, modes):
    blocks = jnp.einsum('ai,...ijk->...ajk', modes[0], blocks, precision=highest)
    blocks = jnp.einsum('bj,...ajk->...abk', modes[1], blocks, precision=highest)
    return jnp.einsum('ck,...abk->...abc', modes[2], blocks, precision=highest)


def transform_back(blocks, modes):
    blocks = jnp.einsum('ai,...ajk->...ijk', modes[0], blocks, precision=highest)
    blocks = jnp.einsum('bj,...ibk->...ijk', modes[1], blocks, precision=highest)
    return jnp.einsum('ck,...ijc->...ijk', modes[2], blocks, precision=highest)


def face_planes(blocks):
    return jnp.stack([blocks[..., 0, :, :], blocks[..., -1, :, :], blocks[..., :, 0, :],
                      blocks[..., :, -1, :], blocks[..., :, :, 0], blocks[..., :, :, -1]], axis=-3)


def restrict(planes, face_modes):
    partial_rows = jnp.einsum('ka,...fab->...fkb', face_modes[0], planes, precision=highest)
    return jnp.sum(partial_rows * face_modes[1], axis=-1)


def extend(values, face_modes):
    return jnp.einsum('ka,...fkb->...fab', face_modes[0], values[..., None] * face_modes[1], precision=highest)


def add_planes(blocks, planes):
    blocks = blocks.at[..., 0, :, :].add(planes[..., 0, :, :])
    blocks = blocks.at[..., -1, :, :].add(planes[..., 1, :, :])
    blocks = blocks.at[..., :, 0, :].add(planes[..., 2, :, :])
    blocks = blocks.at[..., :, -1, :].add(planes[..., 3, :, :])
    blocks = blocks.at[..., :, :, 0].add(planes[..., 4, :, :])
    blocks = blocks.at[..., :, :, -1].add(planes[..., 5, :, :])
    return blocks


def coarse_apply(coarse, fsai_cols, fsai_blocks):
    table = coarse.reshape(-1, fsai_blocks.shape[2])
    picked = table[fsai_cols]
    image = jnp.einsum('rnij,rnj->ri', fsai_blocks, picked, precision=highest)
    spread = jnp.einsum('rnij,ri->rnj', fsai_blocks, image, precision=highest)
    return jnp.zeros_like(table).at[fsai_cols].add(spread).reshape(-1)


def precondition(residual, fd_weights, fd_modes, face_modes, coarse_map, fsai_cols, fsai_blocks):
    blocks = to_blocks(residual)
    local = transform_back(to_blocks(fd_weights) * transform(blocks, fd_modes), fd_modes)
    coarse_local = restrict(face_planes(blocks), face_modes)
    slots = coarse_map.reshape(-1).astype(jnp.int32)
    coarse = jnp.zeros((NCOARSE,), jnp.float32).at[slots].add(coarse_local.reshape(-1))
    back = coarse_apply(coarse, fsai_cols, fsai_blocks)
    correction = back[slots].reshape(coarse_local.shape)
    return from_blocks(add_planes(local, extend(correction, face_modes)))


def reference(source, capacity, fd_weights, fd_modes, face_modes, coarse_map, fsai_cols, fsai_blocks):
    source = source.reshape(NX, NY, NZ)
    capacity = capacity.reshape(NX, NY, NZ)
    fd_weights = fd_weights.reshape(NX, NY, NZ)

    def precond_of(vector):
        return precondition(vector, fd_weights, fd_modes, face_modes, coarse_map, fsai_cols, fsai_blocks)

    solution = jnp.zeros_like(source)
    residual = source
    precond = precond_of(residual)
    direction = precond
    gamma = jnp.sum(residual * precond)
    for step in range(ITERS):
        image = operate(direction, capacity)
        alpha = gamma / jnp.sum(direction * image)
        solution = solution + alpha * direction
        residual = residual - alpha * image
        if step + 1 < ITERS:
            precond = precond_of(residual)
            gamma_next = jnp.sum(residual * precond)
            direction = precond + (gamma_next / gamma) * direction
            gamma = gamma_next
    flat = (NX, NY * NZ)
    return solution.reshape(flat), residual.reshape(flat)
```

```python
import functools
import jax
import jax.numpy as jnp
from jax import lax
from jax.experimental import pallas as pl
from jax.experimental.pallas import tpu as pltpu
from jax.sharding import PartitionSpec as P

C = 64
T = 32
CH = 8
f32 = jnp.float32
bf16 = jnp.bfloat16
HI = lax.Precision.HIGHEST
MESH = pl.DeviceIdType.MESH


def nn(a, b):
    return lax.dot_general(a, b, (((1,), (0,)), ((), ())), precision=HI, preferred_element_type=f32)


def nt(a, b):
    return lax.dot_general(a, b, (((1,), (1,)), ((), ())), precision=HI, preferred_element_type=f32)


def mm(a, b):
    return lax.dot_general(a, b, (((1,), (0,)), ((), ())), preferred_element_type=f32)


def mmt(a, b):
    return lax.dot_general(a, b, (((1,), (1,)), ((), ())), preferred_element_type=f32)


def split(x):
    hi = x.astype(bf16)
    return hi, (x - hi.astype(f32)).astype(bf16)


def iota(shape, dim):
    return lax.broadcasted_iota(jnp.int32, shape, dim)


def left3(m):
    hi, lo = split(m)
    return jnp.concatenate([hi, lo, hi], axis=1)


def rows3(x):
    hi, lo = split(x)
    return jnp.concatenate([hi, hi, lo], axis=0)


def lanes_weights(k):
    hi, lo = split(k)
    top = jnp.concatenate([hi, lo], axis=1)
    bottom = jnp.concatenate([hi, jnp.zeros_like(lo)], axis=1)
    return jnp.concatenate([top, bottom], axis=0)


def lane_transform(x, w):
    hi, lo = split(x)
    r = mm(jnp.concatenate([hi, lo], axis=1), w)
    return r[:, :128] + r[:, 128:]


def kernel(nsub, ncg, x_any, modes_any, face_any, map_any, cols_any, cap_any, wt_any, blk_any,
           p_out, img_out, alpha_out,
           x_ref, modes_ref, face_ref, map_ref, cols_ref,
           s_ref, z_ref, w_ref, p_ref, cap_ref, blk_ref, sel_ref, am_ref, kw_ref,
           ag_ref, send1_ref, a2s_ref, a2r_ref, pick_ref, spread_ref,
           hi_ref, his_ref, hj_ref, hjs_ref, cs_ref, cr_ref,
           dsem, ag_s, ag_r, a2_s, a2_r, h_s, h_r, c_s, c_r):
    n = nsub * ncg
    s = lax.axis_index("sub")
    t = lax.axis_index("cgrp")
    me = s * ncg + t

    def peer(o):
        d = lax.rem(me + o, n)
        return d, (lax.div(d, ncg), lax.rem(d, ncg))

    early = []
    for k, (src, dst) in enumerate(((face_any, face_ref), (map_any, map_ref), (x_any, x_ref),
                                    (modes_any, modes_ref), (cols_any, cols_ref),
                                    (wt_any, w_ref), (blk_any, blk_ref), (cap_any, cap_ref))):
        early.append(pltpu.make_async_copy(src, dst, dsem.at[k]))
        early[-1].start()
    fcopy, mcopy, xcopy, ocopy, lcopy, wcopy, bcopy, ccopy = early

    def mirror(v, bits):
        out = v
        for k in range(8):
            if bits >> k & 1:
                out = out + (1 << k) - (2 << k) * lax.rem(lax.div(v, 1 << k), 2)
        return out

    def peers(step):
        if n > 32:
            @pl.loop(1, n)
            def _(o):
                step(*peer(o))
        else:
            pairs = [(a, b) for a in range(nsub) for b in range(ncg) if a or b]
            for a, b in sorted(pairs, key=lambda ab: -(ab[0] + (ab[1] >> 1 & 1) + (ab[1] >> 2 & 1))):
                ds, dt = mirror(s, a), mirror(t, b)
                step(ds * ncg + dt, (ds, dt))

    def arrived(ref, rows, sem):
        part = ref.at[pl.ds(0, n - 1), pl.ds(0, rows)]
        pltpu.make_async_copy(part, part, sem).wait()

    ag_ref[...] = jnp.zeros_like(ag_ref)
    a2r_ref[...] = jnp.zeros_like(a2r_ref)
    barrier = pltpu.get_barrier_semaphore()

    @pl.loop(1, n)
    def _(o):
        _, dev = peer(o)
        pl.semaphore_signal(barrier, inc=1, device_id=dev, device_id_type=MESH)

    lane = iota((1, 128), 1)
    low = lane < 64
    low32 = jnp.broadcast_to(low, (32, 128))
    low64 = jnp.broadcast_to(low, (64, 128))

    def swap(a):
        return pltpu.roll(a, 64, 1)

    @pl.loop(0, 8)
    def _(c):
        r = iota((128, 512), 0)
        col = iota((128, 512), 1) + c * 512
        hit = ((col >> 6) == (r & 63)) & ((col & 63) == 63 * (r >> 6))
        sel_ref[:, pl.ds(pl.multiple_of(c * 512, 512), 512)] = jnp.where(hit, 1.0, 0.0).astype(bf16)

    fcopy.wait()
    mcopy.wait()
    fm0t = face_ref[0]
    fm1t = face_ref[1]
    r64 = iota((64, 64), 0)
    c64 = iota((64, 64), 1)
    eye64 = jnp.where(r64 == c64, 1.0, 0.0)
    qm = jnp.where(c64 == 2 * (r64 & 31) + (r64 >> 5), 1.0, 0.0)
    dup = jnp.where((iota((64, 128), 1) & 63) == iota((64, 128), 0), 1.0, 0.0)
    dupt = jnp.where((iota((128, 64), 0) & 63) == iota((128, 64), 1), 1.0, 0.0)
    eye128 = jnp.where(iota((128, 128), 0) == iota((128, 128), 1), 1.0, 0.0)
    fm0pt = nn(qm, fm0t)
    fm0 = fm0t.T
    fm0p = fm0pt.T
    fm11 = jnp.concatenate([fm1t, fm1t], axis=0).T

    mapf = [(map_ref[f] & 127).astype(f32) for f in range(6)]
    mapf = jnp.concatenate(mapf + [jnp.zeros((2, 128), f32)], axis=0)
    mapt = mmt(eye128.astype(bf16), mapf.astype(bf16))
    lanef = iota((128, 128), 1).astype(f32)

    xcopy.wait()
    for q in range(T):
        s_ref[q * 8 : q * 8 + 8, :] = x_ref[0:8, q * 128 : q * 128 + 128]
        s_ref[256 + q * 8 : 256 + q * 8 + 8, :] = x_ref[56:64, q * 128 : q * 128 + 128]
    y0 = s_ref[pl.ds(0, 32, stride=8), :]
    y1 = s_ref[pl.ds(263, 32, stride=8), :]
    f01 = jnp.concatenate([jnp.where(low32, y0, swap(y1)), jnp.where(low32, swap(y0), y1)], axis=0)
    f23 = jnp.where(low64, x_ref[:, :128], x_ref[:, 31 * 128 :])
    xh, xl = split(x_ref[...])
    f45 = mmt(jnp.concatenate([xh, xl], axis=0), sel_ref[...])
    f45 = f45[:64] + f45[64:]

    rows = []
    for pair, (left, plane) in enumerate(((fm0p, f01), (fm0, f23), (fm0, f45))):
        u = mm(left3(left), rows3(plane)) * fm11
        for half in range(2):
            keep = low if half == 0 else jnp.logical_not(low)
            val = jnp.sum(jnp.where(keep, u, 0.0), axis=1, keepdims=True)
            f = 2 * pair + half
            place = mapt[:, f : f + 1] == lanef
            rows.append(jnp.sum(jnp.where(place, val, 0.0), axis=0, keepdims=True))
    mine = jnp.concatenate(rows + [jnp.zeros((2, 128), f32)], axis=0)
    send1_ref[...] = mine
    ag_ref[me] = mine

    pl.semaphore_wait(barrier, n - 1)

    @peers
    def _(dd, dev):
        pltpu.make_async_remote_copy(src_ref=send1_ref.at[pl.ds(0, 6)], dst_ref=ag_ref.at[me, pl.ds(0, 6)],
                                     send_sem=ag_s, recv_sem=ag_r,
                                     device_id=dev, device_id_type=MESH).start()

    ocopy.wait()
    m0, m1, m2 = modes_ref[0], modes_ref[1], modes_ref[2]
    am_ref[0] = left3(m0)
    am_ref[1] = left3(nt(eye64, m0))
    am_ref[2] = left3(nt(nn(qm, m1), qm))
    am_ref[3] = left3(nt(nt(qm, m1), qm))
    block = (iota((128, 128), 0) >> 6) == (iota((128, 128), 1) >> 6)
    kw_ref[0] = lanes_weights(jnp.where(block, nn(nt(dupt, m2), dup), 0.0))
    kw_ref[1] = lanes_weights(jnp.where(block, nn(dupt, nn(m2, dup)), 0.0))

    @pl.loop(0, T // CH)
    def _(c):
        base = pl.multiple_of(c * (CH * 128), CH * 128)
        y = mm(am_ref[0], rows3(x_ref[:, pl.ds(base, CH * 128)]))
        stacked = jnp.concatenate([y[:, g * 128 : g * 128 + 128] for g in range(CH)], axis=0)
        s_ref[pl.ds(pl.multiple_of(c * (CH * 64), CH * 64), CH * 64), :] = lane_transform(stacked, kw_ref[0])

    wcopy.wait()
    for q in range(T):
        z_ref[q * 64 : q * 64 + 64, :] = w_ref[:, q * 128 : q * 128 + 128]

    def turned(ref, u):
        a = ref[pl.ds(u, 32, stride=64), :]
        b = ref[pl.ds(u + 32, 32, stride=64), :]
        return jnp.concatenate([jnp.where(low32, a, swap(b)), jnp.where(low32, swap(a), b)], axis=0)

    def middle(c, acc):
        fwd = jnp.concatenate([turned(s_ref, c * CH + g) for g in range(CH)], axis=1)
        wts = jnp.concatenate([turned(z_ref, c * CH + g) for g in range(CH)], axis=1)
        v = mm(am_ref[2], rows3(fwd))
        wv = wts * v
        prod = wv * v
        for g in range(CH):
            acc = acc + prod[:, g * 128 : g * 128 + 128]
        y = mm(am_ref[3], rows3(wv))
        for g in range(CH):
            p_ref[pl.ds(pl.multiple_of(64 + (c * CH + g) * 64, 64), 64), :] = y[:, g * 128 : g * 128 + 128]
        return acc

    gacc = lax.fori_loop(0, T // CH // 2, middle, jnp.zeros((64, 128), f32))

    lcopy.wait()
    cols = cols_ref[...]
    nrow = cols.shape[0]
    nz = cols.shape[1]
    wide_cols = jnp.concatenate([jnp.broadcast_to(cols[i : i + 1, :], (nz, nz)) for i in range(nrow)], axis=0)
    kk = nrow * nz
    pick_diag = iota((kk, nz), 1) == (iota((kk, nz), 0) & (nz - 1))
    colv = jnp.sum(jnp.where(pick_diag, wide_cols.astype(f32), 0.0), axis=1, keepdims=True)
    r = iota((1, n * 8), 1)
    d = r >> 3
    f = r & 7
    own = nrow * d + f
    own = jnp.where((f == 0) & (d >= ncg), nrow * (d - ncg) + 1, own)
    own = jnp.where((f == 2) & (lax.rem(d, ncg) > 0), nrow * (d - 1) + 3, own)
    own = jnp.where(f >= 6, -1, own).astype(f32)
    g1 = jnp.where(colv == own, 1.0, 0.0)
    g1 = jnp.concatenate([g1, jnp.zeros((128 - kk, n * 8), f32)], axis=0)

    g2 = g1.T.astype(bf16)
    g2 = jnp.concatenate([g2, g2], axis=1)
    g1 = g1.astype(bf16)

    arrived(ag_ref, 6, ag_r)
    th, tl = split(ag_ref[...].reshape(n * 8, 128))
    picked = mm(g1, th) + mm(g1, tl)
    pick_ref[...] = picked[:kk].reshape(nrow, nz, 128)
    bcopy.wait()
    spread_ref[...] = jnp.zeros_like(spread_ref)

    def coarse_row(i, acc):
        pk = pick_ref[i]
        tot = blk_ref[i, 0] * pk[0:1]
        for k in range(1, nz):
            tot = tot + blk_ref[i, k] * pk[k : k + 1]
        img = jnp.sum(tot, axis=1, keepdims=True)
        out = [jnp.sum(blk_ref[i, k] * img, axis=0, keepdims=True) for k in range(nz)]
        spread_ref[i] = jnp.concatenate(out, axis=0)
        return acc + img * img

    iacc = lax.fori_loop(0, nrow, coarse_row, jnp.zeros((128, 1), f32))
    back = mm(g2, jnp.concatenate(split(spread_ref[...].reshape(128, 128)), axis=0))
    a2s_ref[...] = back.reshape(n, 8, 128)
    a2r_ref[me] = a2s_ref[me]

    @peers
    def _(dd, dev):
        pltpu.make_async_remote_copy(src_ref=a2s_ref.at[dd, pl.ds(0, 6)], dst_ref=a2r_ref.at[me, pl.ds(0, 6)],
                                     send_sem=a2_s, recv_sem=a2_r,
                                     device_id=dev, device_id_type=MESH).start()

    gacc = lax.fori_loop(T // CH // 2, T // CH, middle, gacc)
    gpart = jnp.sum(iacc, keepdims=True) + jnp.sum(gacc, keepdims=True)

    @pl.loop(0, T // CH)
    def _(c):
        tiles = []
        for g in range(CH):
            a = p_ref[pl.ds(64 + c * CH + g, 32, stride=64), :]
            b = p_ref[pl.ds(96 + c * CH + g, 32, stride=64), :]
            tiles.append(jnp.where(low32, a, swap(b)))
            tiles.append(jnp.where(low32, swap(a), b))
        k = lane_transform(jnp.concatenate(tiles, axis=0), kw_ref[1])
        y = jnp.concatenate([k[g * 64 : g * 64 + 64] for g in range(CH)], axis=1)
        y = mm(am_ref[1], rows3(y))
        for g in range(CH):
            s_ref[pl.ds(pl.multiple_of((c * CH + g) * 64, 64), 64), :] = y[:, g * 128 : g * 128 + 128]

    arrived(a2r_ref, 6, a2_r)
    backs = jnp.sum(a2r_ref[...], axis=0)
    corr = []
    for f in range(6):
        place = mapt[:, f : f + 1] == lanef
        corr.append(jnp.sum(jnp.where(place, backs[f : f + 1], 0.0), axis=1, keepdims=True))
    e01 = mm(left3(fm0pt), rows3(jnp.where(low, corr[0], corr[1]) * fm11))
    e23 = mm(left3(fm0t), rows3(jnp.where(low, corr[2], corr[3]) * fm11))
    e45 = mm(left3(fm0t), rows3(jnp.where(low, corr[4], corr[5]) * fm11))
    eh, el = split(e45)
    eh = jnp.concatenate([eh, el], axis=0)

    @pl.loop(0, T // CH)
    def _(c):
        base = pl.multiple_of(c * (CH * 128), CH * 128)
        add = mm(eh, sel_ref[:, pl.ds(base, CH * 128)])
        for g in range(CH):
            at = pl.multiple_of((c * CH + g) * 64, 64)
            tile = add[:64, g * 128 : g * 128 + 128] + add[64:, g * 128 : g * 128 + 128]
            p_ref[pl.ds(at + 64, 64), :] = s_ref[pl.ds(at, 64), :] + tile

    p_ref[64:128, :] += jnp.where(low64, e23, 0.0)
    p_ref[T * 64 : T * 64 + 64, :] += jnp.where(low64, 0.0, e23)
    top, bottom = e01[:32], e01[32:]
    edge0 = p_ref[pl.ds(64, 32, stride=64), :] + jnp.where(low32, top, swap(bottom))
    edge1 = p_ref[pl.ds(64 + 63, 32, stride=64), :] + jnp.where(low32, swap(top), bottom)
    p_ref[pl.ds(64, 32, stride=64), :] = edge0
    p_ref[pl.ds(64 + 63, 32, stride=64), :] = edge1

    his_ref[0] = edge0
    his_ref[1] = edge1
    hjs_ref[0] = p_ref[64:128, :]
    hjs_ref[1] = p_ref[T * 64 : T * 64 + 64, :]

    sends = (
        (s > 0, s < nsub - 1, (s - 1, t), his_ref, hi_ref, 0, 1, 0),
        (s < nsub - 1, s > 0, (s + 1, t), his_ref, hi_ref, 1, 0, 1),
        (t > 0, t < ncg - 1, (s, t - 1), hjs_ref, hj_ref, 0, 1, 2),
        (t < ncg - 1, t > 0, (s, t + 1), hjs_ref, hj_ref, 1, 0, 3),
    )

    def halo(dev, src, dst, a, b, k):
        return pltpu.make_async_remote_copy(src_ref=src.at[a], dst_ref=dst.at[b], send_sem=h_s.at[k],
                                            recv_sem=h_r.at[k], device_id=dev, device_id_type=MESH)

    for does, gets, dev, src, dst, a, b, k in sends:
        @pl.when(does)
        def _():
            halo(dev, src, dst, a, b, k).start()

        @pl.when(jnp.logical_not(gets))
        def _():
            dst[b] = jnp.zeros(dst.shape[1:], f32)

    ccopy.wait()
    p_ref[0:64, :] = jnp.zeros((64, 128), f32)
    p_ref[(T + 1) * 64 : (T + 2) * 64, :] = jnp.zeros((64, 128), f32)

    row = iota((64, 128), 0)
    kpos = iota((64, 128), 1) & 63

    def stencil(q, acc):
        at = pl.multiple_of(q * 64, 64)
        x = p_ref[pl.ds(at + 64, 64), :]
        here = swap(x)
        before = swap(p_ref[pl.ds(at, 64), :])
        after = swap(p_ref[pl.ds(at + 128, 64), :])
        second = here + jnp.where(low64, before, after)
        up = jnp.where(row == 0, 0.0, pltpu.roll(x, 1, 0))
        down = jnp.where(row == 63, 0.0, pltpu.roll(x, 63, 0))
        third = jnp.where(kpos == 0, 0.0, pltpu.roll(x, 1, 1)) + jnp.where(kpos == 63, 0.0, pltpu.roll(x, 127, 1))
        cols_at = pl.ds(pl.multiple_of(q * 128, 128), 128)
        img = (cap_ref[:, cols_at] + 8.2) * x - (up + down) - 0.6 * second - 2.5 * third
        img_out[:, cols_at] = img
        p_out[:, cols_at] = x
        return acc + x * img

    cacc = lax.fori_loop(0, T, stencil, jnp.zeros((64, 128), f32), unroll=2)
    for does, gets, dev, src, dst, a, b, k in sends:
        @pl.when(gets)
        def _():
            halo(dev, src, dst, a, b, k).wait_recv()

    fix0 = 0.6 * jnp.where(low64, swap(hj_ref[0]), 0.0)
    fix1 = 0.6 * jnp.where(low64, 0.0, swap(hj_ref[1]))
    cacc = cacc - hjs_ref[0] * fix0 - hjs_ref[1] * fix1
    csum = his_ref[0] * hi_ref[0] + his_ref[1] * hi_ref[1]
    cpart = jnp.sum(cacc, axis=0, keepdims=True) - jnp.sum(csum, axis=0, keepdims=True)
    cpart = jnp.where(low, cpart + swap(cpart), gpart * (1.0 / 64.0))
    cs_ref[...] = cpart
    cr_ref[me] = cpart

    @peers
    def _(dd, dev):
        pltpu.make_async_remote_copy(src_ref=cs_ref, dst_ref=cr_ref.at[me], send_sem=c_s, recv_sem=c_r,
                                     device_id=dev, device_id_type=MESH).start()

    img_out[:, :128] = img_out[:, :128] - fix0
    img_out[:, (T - 1) * 128 :] = img_out[:, (T - 1) * 128 :] - fix1
    for q in range(T):
        at = slice(q * 128, q * 128 + 128)
        img_out[0:1, at] = img_out[0:1, at] - hi_ref[0, q : q + 1, :]
        img_out[63:64, at] = img_out[63:64, at] - hi_ref[1, q : q + 1, :]

    pltpu.make_async_copy(cr_ref.at[pl.ds(0, n - 1)], cr_ref.at[pl.ds(0, n - 1)], c_r).wait()
    both = jnp.sum(cr_ref[...], axis=0)
    curv = jnp.sum(jnp.where(low, both, 0.0), axis=1, keepdims=True)
    gamma = jnp.sum(jnp.where(low, 0.0, both), axis=1, keepdims=True)
    alpha_out[...] = gamma / curv

    arrived(ag_ref, 6, ag_s)
    arrived(a2r_ref, 6, a2_s)
    pltpu.make_async_copy(cr_ref.at[pl.ds(0, n - 1)], cr_ref.at[pl.ds(0, n - 1)], c_s).wait()
    for does, gets, dev, src, dst, a, b, k in sends:
        @pl.when(does)
        def _():
            halo(dev, src, dst, a, b, k).wait_send()


def body(nsub, ncg, source, capacity, fd_weights, fd_modes, face_modes, coarse_map, fsai_cols, fsai_blocks):
    n = nsub * ncg
    nrow, nz = fsai_cols.shape
    vm = pl.BlockSpec(memory_space=pltpu.VMEM)
    hbm = pl.BlockSpec(memory_space=pltpu.HBM)
    field = jax.ShapeDtypeStruct(source.shape, f32)
    V = pltpu.VMEM
    dma = pltpu.SemaphoreType.DMA
    p, img, alpha = pl.pallas_call(
        functools.partial(kernel, nsub, ncg),
        out_shape=(field, field, jax.ShapeDtypeStruct((1, 1), f32)),
        in_specs=[hbm] * 8,
        out_specs=(vm, vm, vm),
        scratch_shapes=[
            V(source.shape, f32),
            V(fd_modes.shape, f32),
            V((2, 64, 128), f32),
            V((6, 1, 128), jnp.int32),
            V(fsai_cols.shape, jnp.int32),
            V((T * 64, 128), f32),
            V((T * 64, 128), f32),
            V((64, T * 128), f32),
            V(((T + 2) * 64, 128), f32),
            V((64, T * 128), f32),
            V(fsai_blocks.shape, f32),
            V((128, T * 128), bf16),
            V((4, 64, 192), bf16),
            V((2, 256, 256), bf16),
            V((n, 8, 128), f32),
            V((8, 128), f32),
            V((n, 8, 128), f32),
            V((n, 8, 128), f32),
            V((nrow, nz, 128), f32),
            V((128 // nz, nz, 128), f32),
            V((2, 32, 128), f32),
            V((2, 32, 128), f32),
            V((2, 64, 128), f32),
            V((2, 64, 128), f32),
            V((1, 128), f32),
            V((n, 1, 128), f32),
            dma((8,)),
            dma, dma, dma, dma,
            dma((4,)), dma((4,)),
            dma, dma,
        ],
        compiler_params=pltpu.CompilerParams(collective_id=0, has_side_effects=True,
                                             vmem_limit_bytes=48 * 1024 * 1024),
        cost_estimate=pl.CostEstimate(flops=10**9, bytes_accessed=8 * 2**20, transcendentals=0),
        name="step",
    )(*(pltpu.with_memory_space_constraint(v, pltpu.HBM) for v in (
        source, fd_modes, jnp.swapaxes(face_modes, 1, 2), coarse_map.reshape(-1, 1, coarse_map.shape[-1]),
        fsai_cols, capacity, fd_weights, fsai_blocks)))
    a = alpha[0, 0]
    return a * p, source - a * img


def solution(mesh):
    in_specs = (
        P("sub", "cgrp"),
        P("sub", "cgrp"),
        P("sub", "cgrp"),
        P(),
        P(),
        P("sub", "cgrp", None, None),
        P(("sub", "cgrp"), None),
        P(("sub", "cgrp"), None, None, None),
    )
    out_specs = (P("sub", "cgrp"), P("sub", "cgrp"))
    step = functools.partial(body, mesh.shape["sub"], mesh.shape["cgrp"])
    return jax.shard_map(step, mesh=mesh, in_specs=in_specs, out_specs=out_specs, check_vma=False)
```

```python
import functools
import jax
import jax.numpy as jnp
from jax import lax
from jax.experimental import pallas as pl
from jax.experimental.pallas import tpu as pltpu
from jax.sharding import PartitionSpec as P

C = 64
T = 32
CH = 8
f32 = jnp.float32
bf16 = jnp.bfloat16
HI = lax.Precision.HIGHEST
MESH = pl.DeviceIdType.MESH


def nn(a, b):
    return lax.dot_general(a, b, (((1,), (0,)), ((), ())), precision=HI, preferred_element_type=f32)


def nt(a, b):
    return lax.dot_general(a, b, (((1,), (1,)), ((), ())), precision=HI, preferred_element_type=f32)


def mm(a, b):
    return lax.dot_general(a, b, (((1,), (0,)), ((), ())), preferred_element_type=f32)


def mmt(a, b):
    return lax.dot_general(a, b, (((1,), (1,)), ((), ())), preferred_element_type=f32)


def split(x):
    hi = x.astype(bf16)
    return hi, (x - hi.astype(f32)).astype(bf16)


def iota(shape, dim):
    return lax.broadcasted_iota(jnp.int32, shape, dim)


def left3(m):
    hi, lo = split(m)
    return jnp.concatenate([hi, lo, hi], axis=1)


def rows3(x):
    hi, lo = split(x)
    return jnp.concatenate([hi, hi, lo], axis=0)


def lanes_weights(k):
    hi, lo = split(k)
    top = jnp.concatenate([hi, lo], axis=1)
    bottom = jnp.concatenate([hi, jnp.zeros_like(lo)], axis=1)
    return jnp.concatenate([top, bottom], axis=0)


def lane_transform(x, w):
    hi, lo = split(x)
    r = mm(jnp.concatenate([hi, lo], axis=1), w)
    return r[:, :128] + r[:, 128:]


def kernel(nsub, ncg, x_any, modes_any, face_any, map_any, cols_any, cap_any, wt_any, blk_any,
           p_out, img_out, x_ref, alpha_out,
           modes_ref, face_ref, map_ref, cols_ref,
           s_ref, z_ref, w_ref, p_ref, cap_ref, blk_ref, sel_ref, am_ref, kw_ref,
           ag_ref, send1_ref, a2s_ref, a2r_ref, pick_ref, spread_ref,
           hi_ref, his_ref, hj_ref, hjs_ref, cs_ref, cr_ref,
           dsem, ag_s, ag_r, a2_s, a2_r, h_s, h_r, c_s, c_r):
    n = nsub * ncg
    s = lax.axis_index("sub")
    t = lax.axis_index("cgrp")
    me = s * ncg + t

    def peer(o):
        d = lax.rem(me + o, n)
        return d, (lax.div(d, ncg), lax.rem(d, ncg))

    early = [pltpu.make_async_copy(src, dst, dsem.at[k]) for k, (src, dst) in enumerate((
        (x_any, x_ref), (face_any, face_ref), (map_any, map_ref), (modes_any, modes_ref), (cols_any, cols_ref),
        (wt_any, w_ref), (blk_any, blk_ref), (cap_any, cap_ref)))]
    for copy in early[:5]:
        copy.start()
    xcopy, fcopy, mcopy, ocopy, lcopy, wcopy, bcopy, ccopy = early

    def mirror(v, bits):
        out = v
        for k in range(8):
            if bits >> k & 1:
                out = out + (1 << k) - (2 << k) * lax.rem(lax.div(v, 1 << k), 2)
        return out

    def peers(step):
        if n > 32:
            @pl.loop(1, n)
            def _(o):
                step(*peer(o))
        else:
            pairs = [(a, b) for a in range(nsub) for b in range(ncg) if a or b]
            for a, b in sorted(pairs, key=lambda ab: -(ab[0] + (ab[1] >> 1 & 1) + (ab[1] >> 2 & 1))):
                ds, dt = mirror(s, a), mirror(t, b)
                step(ds * ncg + dt, (ds, dt))

    def arrived(ref, rows, sem):
        part = ref.at[pl.ds(0, n - 1), pl.ds(0, rows)]
        pltpu.make_async_copy(part, part, sem).wait()

    ag_ref[...] = jnp.zeros_like(ag_ref)
    a2r_ref[...] = jnp.zeros_like(a2r_ref)
    barrier = pltpu.get_barrier_semaphore()

    @pl.loop(1, n)
    def _(o):
        _, dev = peer(o)
        pl.semaphore_signal(barrier, inc=1, device_id=dev, device_id_type=MESH)

    lane = iota((1, 128), 1)
    low = lane < 64
    low32 = jnp.broadcast_to(low, (32, 128))
    low64 = jnp.broadcast_to(low, (64, 128))

    def swap(a):
        return pltpu.roll(a, 64, 1)

    @pl.loop(0, 8)
    def _(c):
        r = iota((128, 512), 0)
        col = iota((128, 512), 1) + c * 512
        hit = ((col >> 6) == (r & 63)) & ((col & 63) == 63 * (r >> 6))
        sel_ref[:, pl.ds(pl.multiple_of(c * 512, 512), 512)] = jnp.where(hit, 1.0, 0.0).astype(bf16)

    fcopy.wait()
    mcopy.wait()
    fm0t = face_ref[0]
    fm1t = face_ref[1]
    r64 = iota((64, 64), 0)
    c64 = iota((64, 64), 1)
    eye64 = jnp.where(r64 == c64, 1.0, 0.0)
    qm = jnp.where(c64 == 2 * (r64 & 31) + (r64 >> 5), 1.0, 0.0)
    dup = jnp.where((iota((64, 128), 1) & 63) == iota((64, 128), 0), 1.0, 0.0)
    dupt = jnp.where((iota((128, 64), 0) & 63) == iota((128, 64), 1), 1.0, 0.0)
    eye128 = jnp.where(iota((128, 128), 0) == iota((128, 128), 1), 1.0, 0.0)
    fm0pt = nn(qm, fm0t)
    fm0 = fm0t.T
    fm0p = fm0pt.T
    fm11 = jnp.concatenate([fm1t, fm1t], axis=0).T

    mapf = [(map_ref[f] & 127).astype(f32) for f in range(6)]
    mapf = jnp.concatenate(mapf + [jnp.zeros((2, 128), f32)], axis=0)
    mapt = mmt(eye128.astype(bf16), mapf.astype(bf16))
    lanef = iota((128, 128), 1).astype(f32)

    xcopy.wait()
    for copy in early[5:]:
        copy.start()
    for q in range(T):
        s_ref[q * 8 : q * 8 + 8, :] = x_ref[0:8, q * 128 : q * 128 + 128]
        s_ref[256 + q * 8 : 256 + q * 8 + 8, :] = x_ref[56:64, q * 128 : q * 128 + 128]
    y0 = s_ref[pl.ds(0, 32, stride=8), :]
    y1 = s_ref[pl.ds(263, 32, stride=8), :]
    f01 = jnp.concatenate([jnp.where(low32, y0, swap(y1)), jnp.where(low32, swap(y0), y1)], axis=0)
    f23 = jnp.where(low64, x_ref[:, :128], x_ref[:, 31 * 128 :])
    xh, xl = split(x_ref[...])
    f45 = mmt(jnp.concatenate([xh, xl], axis=0), sel_ref[...])
    f45 = f45[:64] + f45[64:]

    rows = []
    for pair, (left, plane) in enumerate(((fm0p, f01), (fm0, f23), (fm0, f45))):
        u = mm(left3(left), rows3(plane)) * fm11
        for half in range(2):
            keep = low if half == 0 else jnp.logical_not(low)
            val = jnp.sum(jnp.where(keep, u, 0.0), axis=1, keepdims=True)
            f = 2 * pair + half
            place = mapt[:, f : f + 1] == lanef
            rows.append(jnp.sum(jnp.where(place, val, 0.0), axis=0, keepdims=True))
    mine = jnp.concatenate(rows + [jnp.zeros((2, 128), f32)], axis=0)
    send1_ref[...] = mine
    ag_ref[me] = mine

    pl.semaphore_wait(barrier, n - 1)

    @peers
    def _(dd, dev):
        pltpu.make_async_remote_copy(src_ref=send1_ref.at[pl.ds(0, 6)], dst_ref=ag_ref.at[me, pl.ds(0, 6)],
                                     send_sem=ag_s, recv_sem=ag_r,
                                     device_id=dev, device_id_type=MESH).start()

    ocopy.wait()
    m0, m1, m2 = modes_ref[0], modes_ref[1], modes_ref[2]
    am_ref[0] = left3(m0)
    am_ref[1] = left3(nt(eye64, m0))
    am_ref[2] = left3(nt(nn(qm, m1), qm))
    am_ref[3] = left3(nt(nt(qm, m1), qm))
    block = (iota((128, 128), 0) >> 6) == (iota((128, 128), 1) >> 6)
    kw_ref[0] = lanes_weights(jnp.where(block, nn(nt(dupt, m2), dup), 0.0))
    kw_ref[1] = lanes_weights(jnp.where(block, nn(dupt, nn(m2, dup)), 0.0))

    for c in range(T // CH):
        base = (c * (CH * 128))
        y = mm(am_ref[0], rows3(x_ref[:, pl.ds(base, CH * 128)]))
        stacked = jnp.concatenate([y[:, g * 128 : g * 128 + 128] for g in range(CH)], axis=0)
        s_ref[pl.ds((c * (CH * 64)), CH * 64), :] = lane_transform(stacked, kw_ref[0])

    wcopy.wait()
    for q in range(T):
        z_ref[q * 64 : q * 64 + 64, :] = w_ref[:, q * 128 : q * 128 + 128]

    def turned(ref, u):
        a = ref[pl.ds(u, 32, stride=64), :]
        b = ref[pl.ds(u + 32, 32, stride=64), :]
        return jnp.concatenate([jnp.where(low32, a, swap(b)), jnp.where(low32, swap(a), b)], axis=0)

    def middle(c, acc):
        fwd = jnp.concatenate([turned(s_ref, c * CH + g) for g in range(CH)], axis=1)
        wts = jnp.concatenate([turned(z_ref, c * CH + g) for g in range(CH)], axis=1)
        v = mm(am_ref[2], rows3(fwd))
        wv = wts * v
        prod = wv * v
        for g in range(CH):
            acc = acc + prod[:, g * 128 : g * 128 + 128]
        y = mm(am_ref[3], rows3(wv))
        for g in range(CH):
            p_ref[pl.ds((64 + (c * CH + g) * 64), 64), :] = y[:, g * 128 : g * 128 + 128]
        return acc

    gacc = jnp.zeros((64, 128), f32)
    for c in range(T // CH // 2):
        gacc = middle(c, gacc)

    lcopy.wait()
    cols = cols_ref[...]
    nrow = cols.shape[0]
    nz = cols.shape[1]
    wide_cols = jnp.concatenate([jnp.broadcast_to(cols[i : i + 1, :], (nz, nz)) for i in range(nrow)], axis=0)
    kk = nrow * nz
    pick_diag = iota((kk, nz), 1) == (iota((kk, nz), 0) & (nz - 1))
    colv = jnp.sum(jnp.where(pick_diag, wide_cols.astype(f32), 0.0), axis=1, keepdims=True)
    r = iota((1, n * 8), 1)
    d = r >> 3
    f = r & 7
    own = nrow * d + f
    own = jnp.where((f == 0) & (d >= ncg), nrow * (d - ncg) + 1, own)
    own = jnp.where((f == 2) & (lax.rem(d, ncg) > 0), nrow * (d - 1) + 3, own)
    own = jnp.where(f >= 6, -1, own).astype(f32)
    g1 = jnp.where(colv == own, 1.0, 0.0)
    g1 = jnp.concatenate([g1, jnp.zeros((128 - kk, n * 8), f32)], axis=0)

    g2 = g1.T.astype(bf16)
    g2 = jnp.concatenate([g2, g2], axis=1)
    g1 = g1.astype(bf16)

    arrived(ag_ref, 6, ag_r)
    th, tl = split(ag_ref[...].reshape(n * 8, 128))
    picked = mm(g1, th) + mm(g1, tl)
    pick_ref[...] = picked[:kk].reshape(nrow, nz, 128)
    bcopy.wait()
    spread_ref[...] = jnp.zeros_like(spread_ref)

    def coarse_row(i, acc):
        pk = pick_ref[i]
        tot = blk_ref[i, 0] * pk[0:1]
        for k in range(1, nz):
            tot = tot + blk_ref[i, k] * pk[k : k + 1]
        img = jnp.sum(tot, axis=1, keepdims=True)
        out = [jnp.sum(blk_ref[i, k] * img, axis=0, keepdims=True) for k in range(nz)]
        spread_ref[i] = jnp.concatenate(out, axis=0)
        return acc + img * img

    iacc = lax.fori_loop(0, nrow, coarse_row, jnp.zeros((128, 1), f32))
    back = mm(g2, jnp.concatenate(split(spread_ref[...].reshape(128, 128)), axis=0))
    a2s_ref[...] = back.reshape(n, 8, 128)
    a2r_ref[me] = a2s_ref[me]

    @peers
    def _(dd, dev):
        pltpu.make_async_remote_copy(src_ref=a2s_ref.at[dd, pl.ds(0, 6)], dst_ref=a2r_ref.at[me, pl.ds(0, 6)],
                                     send_sem=a2_s, recv_sem=a2_r,
                                     device_id=dev, device_id_type=MESH).start()

    for c in range(T // CH // 2, T // CH):
        gacc = middle(c, gacc)
    gpart = jnp.sum(iacc, keepdims=True) + jnp.sum(gacc, keepdims=True)

    for c in range(T // CH):
        tiles = []
        for g in range(CH):
            a = p_ref[pl.ds(64 + c * CH + g, 32, stride=64), :]
            b = p_ref[pl.ds(96 + c * CH + g, 32, stride=64), :]
            tiles.append(jnp.where(low32, a, swap(b)))
            tiles.append(jnp.where(low32, swap(a), b))
        k = lane_transform(jnp.concatenate(tiles, axis=0), kw_ref[1])
        y = jnp.concatenate([k[g * 64 : g * 64 + 64] for g in range(CH)], axis=1)
        y = mm(am_ref[1], rows3(y))
        for g in range(CH):
            s_ref[pl.ds(((c * CH + g) * 64), 64), :] = y[:, g * 128 : g * 128 + 128]

    arrived(a2r_ref, 6, a2_r)
    backs = jnp.sum(a2r_ref[...], axis=0)
    corr = []
    for f in range(6):
        place = mapt[:, f : f + 1] == lanef
        corr.append(jnp.sum(jnp.where(place, backs[f : f + 1], 0.0), axis=1, keepdims=True))
    e01 = mm(left3(fm0pt), rows3(jnp.where(low, corr[0], corr[1]) * fm11))
    e23 = mm(left3(fm0t), rows3(jnp.where(low, corr[2], corr[3]) * fm11))
    e45 = mm(left3(fm0t), rows3(jnp.where(low, corr[4], corr[5]) * fm11))
    eh, el = split(e45)
    eh = jnp.concatenate([eh, el], axis=0)

    for c in range(T // CH):
        base = (c * (CH * 128))
        add = mm(eh, sel_ref[:, pl.ds(base, CH * 128)])
        for g in range(CH):
            at = ((c * CH + g) * 64)
            tile = add[:64, g * 128 : g * 128 + 128] + add[64:, g * 128 : g * 128 + 128]
            p_ref[pl.ds(at + 64, 64), :] = s_ref[pl.ds(at, 64), :] + tile

    p_ref[64:128, :] += jnp.where(low64, e23, 0.0)
    p_ref[T * 64 : T * 64 + 64, :] += jnp.where(low64, 0.0, e23)
    top, bottom = e01[:32], e01[32:]
    edge0 = p_ref[pl.ds(64, 32, stride=64), :] + jnp.where(low32, top, swap(bottom))
    edge1 = p_ref[pl.ds(64 + 63, 32, stride=64), :] + jnp.where(low32, swap(top), bottom)
    p_ref[pl.ds(64, 32, stride=64), :] = edge0
    p_ref[pl.ds(64 + 63, 32, stride=64), :] = edge1

    his_ref[0] = edge0
    his_ref[1] = edge1
    hjs_ref[0] = p_ref[64:128, :]
    hjs_ref[1] = p_ref[T * 64 : T * 64 + 64, :]

    sends = (
        (s > 0, s < nsub - 1, (s - 1, t), his_ref, hi_ref, 0, 1, 0),
        (s < nsub - 1, s > 0, (s + 1, t), his_ref, hi_ref, 1, 0, 1),
        (t > 0, t < ncg - 1, (s, t - 1), hjs_ref, hj_ref, 0, 1, 2),
        (t < ncg - 1, t > 0, (s, t + 1), hjs_ref, hj_ref, 1, 0, 3),
    )

    def halo(dev, src, dst, a, b, k):
        return pltpu.make_async_remote_copy(src_ref=src.at[a], dst_ref=dst.at[b], send_sem=h_s.at[k],
                                            recv_sem=h_r.at[k], device_id=dev, device_id_type=MESH)

    for does, gets, dev, src, dst, a, b, k in sends:
        @pl.when(does)
        def _():
            halo(dev, src, dst, a, b, k).start()

        @pl.when(jnp.logical_not(gets))
        def _():
            dst[b] = jnp.zeros(dst.shape[1:], f32)

    ccopy.wait()
    p_ref[0:64, :] = jnp.zeros((64, 128), f32)
    p_ref[(T + 1) * 64 : (T + 2) * 64, :] = jnp.zeros((64, 128), f32)

    row = iota((64, 128), 0)
    kpos = iota((64, 128), 1) & 63

    def stencil(q, acc):
        at = pl.multiple_of(q * 64, 64)
        x = p_ref[pl.ds(at + 64, 64), :]
        second = swap(x + jnp.where(low64, p_ref[pl.ds(at + 128, 64), :], p_ref[pl.ds(at, 64), :]))
        up = jnp.where(row == 0, 0.0, pltpu.roll(x, 1, 0))
        down = jnp.where(row == 63, 0.0, pltpu.roll(x, 63, 0))
        third = jnp.where(kpos == 0, 0.0, pltpu.roll(x, 1, 1)) + jnp.where(kpos == 63, 0.0, pltpu.roll(x, 127, 1))
        cols_at = pl.ds(pl.multiple_of(q * 128, 128), 128)
        img = (cap_ref[:, cols_at] + 8.2) * x - (up + down) - 0.6 * second - 2.5 * third
        img_out[:, cols_at] = img
        p_out[:, cols_at] = x
        return acc + x * img

    cacc = lax.fori_loop(0, T, stencil, jnp.zeros((64, 128), f32), unroll=4)
    for does, gets, dev, src, dst, a, b, k in sends:
        @pl.when(gets)
        def _():
            halo(dev, src, dst, a, b, k).wait_recv()

    fix0 = 0.6 * jnp.where(low64, swap(hj_ref[0]), 0.0)
    fix1 = 0.6 * jnp.where(low64, 0.0, swap(hj_ref[1]))
    cacc = cacc - hjs_ref[0] * fix0 - hjs_ref[1] * fix1
    csum = his_ref[0] * hi_ref[0] + his_ref[1] * hi_ref[1]
    cpart = jnp.sum(cacc, axis=0, keepdims=True) - jnp.sum(csum, axis=0, keepdims=True)
    cpart = jnp.where(low, cpart + swap(cpart), gpart * (1.0 / 64.0))
    cs_ref[...] = cpart
    cr_ref[me] = cpart

    @peers
    def _(dd, dev):
        pltpu.make_async_remote_copy(src_ref=cs_ref, dst_ref=cr_ref.at[me], send_sem=c_s, recv_sem=c_r,
                                     device_id=dev, device_id_type=MESH).start()

    img_out[:, :128] = img_out[:, :128] - fix0
    img_out[:, (T - 1) * 128 :] = img_out[:, (T - 1) * 128 :] - fix1
    for q in range(T):
        at = slice(q * 128, q * 128 + 128)
        img_out[0:1, at] = img_out[0:1, at] - hi_ref[0, q : q + 1, :]
        img_out[63:64, at] = img_out[63:64, at] - hi_ref[1, q : q + 1, :]

    pltpu.make_async_copy(cr_ref.at[pl.ds(0, n - 1)], cr_ref.at[pl.ds(0, n - 1)], c_r).wait()
    both = jnp.sum(cr_ref[...], axis=0)
    curv = jnp.sum(jnp.where(low, both, 0.0), axis=1, keepdims=True)
    gamma = jnp.sum(jnp.where(low, 0.0, both), axis=1, keepdims=True)
    alpha_out[...] = gamma / curv

    arrived(ag_ref, 6, ag_s)
    arrived(a2r_ref, 6, a2_s)
    pltpu.make_async_copy(cr_ref.at[pl.ds(0, n - 1)], cr_ref.at[pl.ds(0, n - 1)], c_s).wait()
    for does, gets, dev, src, dst, a, b, k in sends:
        @pl.when(does)
        def _():
            halo(dev, src, dst, a, b, k).wait_send()


def finish(p_ref, img_ref, x_ref, alpha_ref, sol_any, res_any, sol_ref, res_ref, sem):
    copies = []
    a = alpha_ref[...]
    for c in range(8):
        at = pl.ds(c * 8, 8)
        sol_ref[at, :] = a * p_ref[at, :]
        copies.append(pltpu.make_async_copy(sol_ref.at[at], sol_any.at[at], sem.at[0, c]))
        copies[-1].start()
        res_ref[at, :] = x_ref[at, :] - a * img_ref[at, :]
        copies.append(pltpu.make_async_copy(res_ref.at[at], res_any.at[at], sem.at[1, c]))
        copies[-1].start()
    for copy in copies:
        copy.wait()


def body(nsub, ncg, source, capacity, fd_weights, fd_modes, face_modes, coarse_map, fsai_cols, fsai_blocks):
    n = nsub * ncg
    nrow, nz = fsai_cols.shape
    vm = pl.BlockSpec(memory_space=pltpu.VMEM)
    hbm = pl.BlockSpec(memory_space=pltpu.HBM)
    field = jax.ShapeDtypeStruct(source.shape, f32)
    V = pltpu.VMEM
    dma = pltpu.SemaphoreType.DMA
    p, img, x, alpha = pl.pallas_call(
        functools.partial(kernel, nsub, ncg),
        out_shape=(field, field, field, jax.ShapeDtypeStruct((1, 1), f32)),
        in_specs=[hbm] * 8,
        out_specs=(vm, vm, vm, vm),
        scratch_shapes=[
            V(fd_modes.shape, f32),
            V((2, 64, 128), f32),
            V((6, 1, 128), jnp.int32),
            V(fsai_cols.shape, jnp.int32),
            V((T * 64, 128), f32),
            V((T * 64, 128), f32),
            V((64, T * 128), f32),
            V(((T + 2) * 64, 128), f32),
            V((64, T * 128), f32),
            V(fsai_blocks.shape, f32),
            V((128, T * 128), bf16),
            V((4, 64, 192), bf16),
            V((2, 256, 256), bf16),
            V((n, 8, 128), f32),
            V((8, 128), f32),
            V((n, 8, 128), f32),
            V((n, 8, 128), f32),
            V((nrow, nz, 128), f32),
            V((128 // nz, nz, 128), f32),
            V((2, 32, 128), f32),
            V((2, 32, 128), f32),
            V((2, 64, 128), f32),
            V((2, 64, 128), f32),
            V((1, 128), f32),
            V((n, 1, 128), f32),
            dma((8,)),
            dma, dma, dma, dma,
            dma((4,)), dma((4,)),
            dma, dma,
        ],
        compiler_params=pltpu.CompilerParams(collective_id=0, has_side_effects=True,
                                             vmem_limit_bytes=48 * 1024 * 1024),
        cost_estimate=pl.CostEstimate(flops=10**9, bytes_accessed=8 * 2**20, transcendentals=0),
        name="step",
    )(*(pltpu.with_memory_space_constraint(v, pltpu.HBM) for v in (
        source, fd_modes, jnp.swapaxes(face_modes, 1, 2), coarse_map.reshape(-1, 1, coarse_map.shape[-1]),
        fsai_cols, capacity, fd_weights, fsai_blocks)))
    return pl.pallas_call(
        finish,
        out_shape=(field, field),
        in_specs=[vm] * 4,
        out_specs=(hbm, hbm),
        scratch_shapes=[V(source.shape, f32), V(source.shape, f32), dma((2, 8))],
        cost_estimate=pl.CostEstimate(flops=2**20, bytes_accessed=2 * 2**20, transcendentals=0),
        name="finish",
    )(*(pltpu.with_memory_space_constraint(v, pltpu.VMEM) for v in (p, img, x, alpha)))


def solution(mesh):
    in_specs = (
        P("sub", "cgrp"),
        P("sub", "cgrp"),
        P("sub", "cgrp"),
        P(),
        P(),
        P("sub", "cgrp", None, None),
        P(("sub", "cgrp"), None),
        P(("sub", "cgrp"), None, None, None),
    )
    out_specs = (P("sub", "cgrp"), P("sub", "cgrp"))
    step = functools.partial(body, mesh.shape["sub"], mesh.shape["cgrp"])
    return jax.shard_map(step, mesh=mesh, in_specs=in_specs, out_specs=out_specs, check_vma=False)
```

```python
import functools
import jax
import jax.numpy as jnp
from jax import lax
from jax.experimental import pallas as pl
from jax.experimental.pallas import tpu as pltpu
from jax.sharding import PartitionSpec as P

C = 64
T = 32
CH = 8
f32 = jnp.float32
bf16 = jnp.bfloat16
HI = lax.Precision.HIGHEST
MESH = pl.DeviceIdType.MESH


def nn(a, b):
    return lax.dot_general(a, b, (((1,), (0,)), ((), ())), precision=HI, preferred_element_type=f32)


def nt(a, b):
    return lax.dot_general(a, b, (((1,), (1,)), ((), ())), precision=HI, preferred_element_type=f32)


def mm(a, b):
    return lax.dot_general(a, b, (((1,), (0,)), ((), ())), preferred_element_type=f32)


def mmt(a, b):
    return lax.dot_general(a, b, (((1,), (1,)), ((), ())), preferred_element_type=f32)


def split(x):
    hi = x.astype(bf16)
    return hi, (x - hi.astype(f32)).astype(bf16)


def iota(shape, dim):
    return lax.broadcasted_iota(jnp.int32, shape, dim)


def left3(m):
    hi, lo = split(m)
    return jnp.concatenate([hi, lo, hi], axis=1)


def rows3(x):
    hi, lo = split(x)
    return jnp.concatenate([hi, hi, lo], axis=0)


def lanes_weights(k):
    hi, lo = split(k)
    top = jnp.concatenate([hi, lo], axis=1)
    bottom = jnp.concatenate([hi, jnp.zeros_like(lo)], axis=1)
    return jnp.concatenate([top, bottom], axis=0)


def lane_transform(x, w):
    hi, lo = split(x)
    r = mm(jnp.concatenate([hi, lo], axis=1), w)
    return r[:, :128] + r[:, 128:]


def kernel(nsub, ncg, x_any, modes_any, face_any, map_any, cols_any, cap_any, wt_any, blk_any,
           p_out, img_out, x_ref, alpha_out,
           modes_ref, face_ref, map_ref, cols_ref,
           s_ref, z_ref, w_ref, p_ref, cap_ref, blk_ref, sel_ref, am_ref, kw_ref,
           ag_ref, send1_ref, a2s_ref, a2r_ref, pick_ref, spread_ref,
           hi_ref, his_ref, hj_ref, hjs_ref, cs_ref, cr_ref, l_ref, strip_ref,
           dsem, ag_s, ag_r, a2_s, a2_r, h_s, h_r, c_s, c_r):
    n = nsub * ncg
    s = lax.axis_index("sub")
    t = lax.axis_index("cgrp")
    me = s * ncg + t

    def peer(o):
        d = lax.rem(me + o, n)
        return d, (lax.div(d, ncg), lax.rem(d, ncg))

    early = [pltpu.make_async_copy(src, dst, dsem.at[k]) for k, (src, dst) in enumerate((
        (x_any, x_ref), (face_any, face_ref), (map_any, map_ref), (modes_any, modes_ref), (cols_any, cols_ref),
        (wt_any, w_ref), (blk_any, blk_ref), (cap_any, cap_ref)))]
    for copy in early[:5]:
        copy.start()
    xcopy, fcopy, mcopy, ocopy, lcopy, wcopy, bcopy, ccopy = early

    def mirror(v, bits):
        out = v
        for k in range(8):
            if bits >> k & 1:
                out = out + (1 << k) - (2 << k) * lax.rem(lax.div(v, 1 << k), 2)
        return out

    def peers(step):
        if n > 32:
            @pl.loop(1, n)
            def _(o):
                step(*peer(o))
        else:
            pairs = [(a, b) for a in range(nsub) for b in range(ncg) if a or b]
            for a, b in sorted(pairs, key=lambda ab: -(ab[0] + (ab[1] >> 1 & 1) + (ab[1] >> 2 & 1))):
                ds, dt = mirror(s, a), mirror(t, b)
                step(ds * ncg + dt, (ds, dt))

    def arrived(ref, rows, sem):
        part = ref.at[pl.ds(0, n - 1), pl.ds(0, rows)]
        pltpu.make_async_copy(part, part, sem).wait()

    ag_ref[...] = jnp.zeros_like(ag_ref)
    a2r_ref[...] = jnp.zeros_like(a2r_ref)
    barrier = pltpu.get_barrier_semaphore()

    @pl.loop(1, n)
    def _(o):
        _, dev = peer(o)
        pl.semaphore_signal(barrier, inc=1, device_id=dev, device_id_type=MESH)

    lane = iota((1, 128), 1)
    low = lane < 64
    low32 = jnp.broadcast_to(low, (32, 128))
    low64 = jnp.broadcast_to(low, (64, 128))

    def swap(a):
        return pltpu.roll(a, 64, 1)

    @pl.loop(0, 8)
    def _(c):
        r = iota((128, 512), 0)
        col = iota((128, 512), 1) + c * 512
        hit = ((col >> 6) == (r & 63)) & ((col & 63) == 63 * (r >> 6))
        sel_ref[:, pl.ds(pl.multiple_of(c * 512, 512), 512)] = jnp.where(hit, 1.0, 0.0).astype(bf16)

    fcopy.wait()
    mcopy.wait()
    fm0t = face_ref[0]
    fm1t = face_ref[1]
    r64 = iota((64, 64), 0)
    c64 = iota((64, 64), 1)
    eye64 = jnp.where(r64 == c64, 1.0, 0.0)
    qm = jnp.where(c64 == 2 * (r64 & 31) + (r64 >> 5), 1.0, 0.0)
    dup = jnp.where((iota((64, 128), 1) & 63) == iota((64, 128), 0), 1.0, 0.0)
    dupt = jnp.where((iota((128, 64), 0) & 63) == iota((128, 64), 1), 1.0, 0.0)
    eye128 = jnp.where(iota((128, 128), 0) == iota((128, 128), 1), 1.0, 0.0)
    fm0pt = nn(qm, fm0t)
    fm0 = fm0t.T
    fm0p = fm0pt.T
    fm11 = jnp.concatenate([fm1t, fm1t], axis=0).T

    mapf = [(map_ref[f] & 127).astype(f32) for f in range(6)]
    mapf = jnp.concatenate(mapf + [jnp.zeros((2, 128), f32)], axis=0)
    mapt = mmt(eye128.astype(bf16), mapf.astype(bf16))
    lanef = iota((128, 128), 1).astype(f32)

    xcopy.wait()
    for copy in early[5:]:
        copy.start()

    def pair(a, b):
        return jnp.concatenate([jnp.where(low32, a, swap(b)), jnp.where(low32, swap(a), b)], axis=0)

    def planes(ref):
        for q in range(T):
            strip_ref[q * 8 : q * 8 + 8, :] = ref[0:8, q * 128 : q * 128 + 128]
            strip_ref[256 + q * 8 : 256 + q * 8 + 8, :] = ref[56:64, q * 128 : q * 128 + 128]
        y0 = strip_ref[pl.ds(0, 32, stride=8), :]
        y1 = strip_ref[pl.ds(263, 32, stride=8), :]
        f01 = pair(y0, y1)
        f23 = jnp.where(low64, ref[:, :128], ref[:, 31 * 128 :])
        f45 = mmt(jnp.concatenate(split(ref[...]), axis=0), sel_ref[...])
        return f01, f23, f45[:64] + f45[64:]

    def restrict(f01, f23, f45):
        vals = []
        for left, plane in ((fm0p, f01), (fm0, f23), (fm0, f45)):
            u = mm(left3(left), rows3(plane)) * fm11
            vals.append(jnp.sum(jnp.where(low, u, 0.0), axis=1, keepdims=True))
            vals.append(jnp.sum(jnp.where(low, 0.0, u), axis=1, keepdims=True))
        return vals

    rows = []
    for f, val in enumerate(restrict(*planes(x_ref))):
        place = mapt[:, f : f + 1] == lanef
        rows.append(jnp.sum(jnp.where(place, val, 0.0), axis=0, keepdims=True))
    mine = jnp.concatenate(rows + [jnp.zeros((2, 128), f32)], axis=0)
    send1_ref[...] = mine
    ag_ref[me] = mine

    pl.semaphore_wait(barrier, n - 1)

    @peers
    def _(dd, dev):
        pltpu.make_async_remote_copy(src_ref=send1_ref.at[pl.ds(0, 6)], dst_ref=ag_ref.at[me, pl.ds(0, 6)],
                                     send_sem=ag_s, recv_sem=ag_r,
                                     device_id=dev, device_id_type=MESH).start()

    ocopy.wait()
    m0, m1, m2 = modes_ref[0], modes_ref[1], modes_ref[2]
    am_ref[0] = left3(m0)
    am_ref[1] = left3(nt(eye64, m0))
    am_ref[2] = left3(nt(nn(qm, m1), qm))
    am_ref[3] = left3(nt(nt(qm, m1), qm))
    block = (iota((128, 128), 0) >> 6) == (iota((128, 128), 1) >> 6)
    kw_ref[0] = lanes_weights(jnp.where(block, nn(nt(dupt, m2), dup), 0.0))
    kw_ref[1] = lanes_weights(jnp.where(block, nn(dupt, nn(m2, dup)), 0.0))

    for c in range(T // CH):
        base = (c * (CH * 128))
        y = mm(am_ref[0], rows3(x_ref[:, pl.ds(base, CH * 128)]))
        stacked = jnp.concatenate([y[:, g * 128 : g * 128 + 128] for g in range(CH)], axis=0)
        s_ref[pl.ds((c * (CH * 64)), CH * 64), :] = lane_transform(stacked, kw_ref[0])

    wcopy.wait()
    for q in range(T):
        z_ref[q * 64 : q * 64 + 64, :] = w_ref[:, q * 128 : q * 128 + 128]

    def turned(ref, u):
        a = ref[pl.ds(u, 32, stride=64), :]
        b = ref[pl.ds(u + 32, 32, stride=64), :]
        return jnp.concatenate([jnp.where(low32, a, swap(b)), jnp.where(low32, swap(a), b)], axis=0)

    def middle(c, acc):
        fwd = jnp.concatenate([turned(s_ref, c * CH + g) for g in range(CH)], axis=1)
        wts = jnp.concatenate([turned(z_ref, c * CH + g) for g in range(CH)], axis=1)
        v = mm(am_ref[2], rows3(fwd))
        wv = wts * v
        prod = wv * v
        for g in range(CH):
            acc = acc + prod[:, g * 128 : g * 128 + 128]
        y = mm(am_ref[3], rows3(wv))
        for g in range(CH):
            p_ref[pl.ds((64 + (c * CH + g) * 64), 64), :] = y[:, g * 128 : g * 128 + 128]
        return acc

    gacc = jnp.zeros((64, 128), f32)
    for c in range(T // CH):
        gacc = middle(c, gacc)

    ccopy.wait()
    cap01, cap23, cap45 = planes(cap_ref)

    lcopy.wait()
    cols = cols_ref[...]
    nrow = cols.shape[0]
    nz = cols.shape[1]
    wide_cols = jnp.concatenate([jnp.broadcast_to(cols[i : i + 1, :], (nz, nz)) for i in range(nrow)], axis=0)
    kk = nrow * nz
    pick_diag = iota((kk, nz), 1) == (iota((kk, nz), 0) & (nz - 1))
    colv = jnp.sum(jnp.where(pick_diag, wide_cols.astype(f32), 0.0), axis=1, keepdims=True)
    r = iota((1, n * 8), 1)
    d = r >> 3
    f = r & 7
    own = nrow * d + f
    own = jnp.where((f == 0) & (d >= ncg), nrow * (d - ncg) + 1, own)
    own = jnp.where((f == 2) & (lax.rem(d, ncg) > 0), nrow * (d - 1) + 3, own)
    own = jnp.where(f >= 6, -1, own).astype(f32)
    g1 = jnp.where(colv == own, 1.0, 0.0)
    g1 = jnp.concatenate([g1, jnp.zeros((128 - kk, n * 8), f32)], axis=0)

    g2 = g1.T.astype(bf16)
    g2 = jnp.concatenate([g2, g2], axis=1)
    g1 = g1.astype(bf16)

    arrived(ag_ref, 6, ag_r)
    th, tl = split(ag_ref[...].reshape(n * 8, 128))
    picked = mm(g1, th) + mm(g1, tl)
    pick_ref[...] = picked[:kk].reshape(nrow, nz, 128)
    bcopy.wait()
    spread_ref[...] = jnp.zeros_like(spread_ref)

    def coarse_row(i, acc):
        pk = pick_ref[i]
        tot = blk_ref[i, 0] * pk[0:1]
        for k in range(1, nz):
            tot = tot + blk_ref[i, k] * pk[k : k + 1]
        img = jnp.sum(tot, axis=1, keepdims=True)
        out = [jnp.sum(blk_ref[i, k] * img, axis=0, keepdims=True) for k in range(nz)]
        spread_ref[i] = jnp.concatenate(out, axis=0)
        return acc + img * img

    iacc = jnp.zeros((128, 1), f32)
    for i in range(nrow):
        iacc = coarse_row(i, iacc)
    back = mm(g2, jnp.concatenate(split(spread_ref[...].reshape(128, 128)), axis=0))
    a2s_ref[...] = back.reshape(n, 8, 128)
    a2r_ref[me] = a2s_ref[me]

    @peers
    def _(dd, dev):
        pltpu.make_async_remote_copy(src_ref=a2s_ref.at[dd, pl.ds(0, 6)], dst_ref=a2r_ref.at[me, pl.ds(0, 6)],
                                     send_sem=a2_s, recv_sem=a2_r,
                                     device_id=dev, device_id_type=MESH).start()

    gpart = jnp.sum(iacc, keepdims=True) + jnp.sum(gacc, keepdims=True)

    for c in range(T // CH):
        tiles = []
        for g in range(CH):
            a = p_ref[pl.ds(64 + c * CH + g, 32, stride=64), :]
            b = p_ref[pl.ds(96 + c * CH + g, 32, stride=64), :]
            tiles.append(jnp.where(low32, a, swap(b)))
            tiles.append(jnp.where(low32, swap(a), b))
        k = lane_transform(jnp.concatenate(tiles, axis=0), kw_ref[1])
        y = jnp.concatenate([k[g * 64 : g * 64 + 64] for g in range(CH)], axis=1)
        y = mm(am_ref[1], rows3(y))
        for g in range(CH):
            l_ref[pl.ds(((c * CH + g) * 64 + 64), 64), :] = y[:, g * 128 : g * 128 + 128]

    row = iota((64, 128), 0)
    kpos = iota((64, 128), 1) & 63

    def operate(ref, q):
        at = q * 64
        x = ref[pl.ds(at + 64, 64), :]
        second = swap(x + jnp.where(low64, ref[pl.ds(at + 128, 64), :], ref[pl.ds(at, 64), :]))
        up = jnp.where(row == 0, 0.0, pltpu.roll(x, 1, 0))
        down = jnp.where(row == 63, 0.0, pltpu.roll(x, 63, 0))
        third = jnp.where(kpos == 0, 0.0, pltpu.roll(x, 1, 1)) + jnp.where(kpos == 63, 0.0, pltpu.roll(x, 127, 1))
        cols_at = pl.ds(q * 128, 128)
        img = (cap_ref[:, cols_at] + 8.2) * x - (up + down) - 0.6 * second - 2.5 * third
        img_out[:, cols_at] = img
        return x, img

    sends = (
        (s > 0, s < nsub - 1, (s - 1, t), his_ref, hi_ref, 0, 1, 0),
        (s < nsub - 1, s > 0, (s + 1, t), his_ref, hi_ref, 1, 0, 1),
        (t > 0, t < ncg - 1, (s, t - 1), hjs_ref, hj_ref, 0, 1, 2),
        (t < ncg - 1, t > 0, (s, t + 1), hjs_ref, hj_ref, 1, 0, 3),
    )

    def halo(turn, dev, src, dst, a, b, k):
        return pltpu.make_async_remote_copy(src_ref=src.at[turn, a], dst_ref=dst.at[turn, b], send_sem=h_s.at[turn, k],
                                            recv_sem=h_r.at[turn, k], device_id=dev, device_id_type=MESH)

    def send_halo(turn, edge0, edge1, ref):
        his_ref[turn, 0] = edge0
        his_ref[turn, 1] = edge1
        hjs_ref[turn, 0] = jnp.where(low32, ref[64:96, :], swap(ref[96:128, :]))
        hjs_ref[turn, 1] = jnp.where(low32, swap(ref[T * 64 : T * 64 + 32, :]), ref[T * 64 + 32 : T * 64 + 64, :])
        for does, gets, dev, src, dst, a, b, k in sends:
            @pl.when(does)
            def _():
                halo(turn, dev, src, dst, a, b, k).start()

            @pl.when(jnp.logical_not(gets))
            def _():
                dst[turn, b] = jnp.zeros(dst.shape[2:], f32)

    def await_halo(turn):
        for does, gets, dev, src, dst, a, b, k in sends:
            @pl.when(gets)
            def _():
                halo(turn, dev, src, dst, a, b, k).wait_recv()

    l_ref[0:64, :] = jnp.zeros((64, 128), f32)
    l_ref[(T + 1) * 64 : (T + 2) * 64, :] = jnp.zeros((64, 128), f32)
    ledge0 = l_ref[pl.ds(64, 32, stride=64), :]
    ledge1 = l_ref[pl.ds(64 + 63, 32, stride=64), :]
    send_halo(0, ledge0, ledge1, l_ref)
    cacc = jnp.zeros((64, 128), f32)
    for q in range(T):
        value, img = operate(l_ref, q)
        cacc = cacc + value * img
    l01 = pair(ledge0, ledge1)
    l23 = jnp.where(low64, l_ref[64:128, :], l_ref[T * 64 : T * 64 + 64, :])
    image_vals = restrict(*planes(img_out))

    fm00 = jnp.concatenate([fm0t, fm0t], axis=0).T
    fm0p3, fm03, fm13, fm1p3 = left3(fm0pt), left3(fm0t), left3(fm1t), left3(nn(qm, fm1t))
    inner_row = (row > 0) & (row < 63)
    inner_col = (kpos > 0) & (kpos < 63)
    last_row = row == 63
    last_col = kpos == 63
    s_low = jnp.where(s > 0, 1.0, 0.0)
    s_high = jnp.where(s < nsub - 1, 1.0, 0.0)
    t_low = jnp.where(t > 0, 0.6, 0.0)
    t_high = jnp.where(t < ncg - 1, 0.6, 0.0)

    arrived(a2r_ref, 6, a2_r)
    backs = jnp.sum(a2r_ref[...], axis=0)
    corr = []
    for f in range(6):
        place = mapt[:, f : f + 1] == lanef
        corr.append(jnp.sum(jnp.where(place, backs[f : f + 1], 0.0), axis=1, keepdims=True))
    c01, c23, c45 = (jnp.where(low, corr[2 * f], corr[2 * f + 1]) for f in range(3))
    e01 = mm(fm0p3, rows3(c01 * fm11))
    e23 = mm(fm03, rows3(c23 * fm11))
    e45 = mm(fm03, rows3(c45 * fm11))
    t01 = mm(fm13, rows3(c01 * fm00))
    t45 = mm(fm1p3, rows3(c45 * fm00))

    def corners(e):
        lanes = iota(e.shape, 1)
        ends = jnp.where((lanes == 0) | (lanes == 127), e, 0.0)
        ends = jnp.where(lanes == 63, pltpu.roll(e, 127, 1), ends)
        return jnp.where(lanes == 64, pltpu.roll(e, 1, 1), ends)

    def whole(e, side, rows):
        first, last = rows[0:1], rows[63:64]
        ends = jnp.where(row == 0, jnp.where(low, first, swap(last)), 0.0)
        ends = jnp.where(row == 63, jnp.where(low, swap(first), last), ends)
        return e + corners(side) + ends

    q01 = whole(e01, t45, e23)
    q23 = whole(e23, e45, e01)
    q45 = whole(e45, e23, t01)
    n01, n23, n45 = (jnp.where(last_col, 0.0, pltpu.roll(v, 127, 1)) for v in (q01, q23, q45))
    d01 = q01 * ((cap01 + 8.2) * q01 - 5.0 * n01)
    d23 = q23 * ((cap23 + 8.2) * q23 - 5.0 * n23)
    d45 = q45 * (jnp.where(inner_col, (cap45 + 8.2) * q45, 0.0) - 1.2 * n45)
    quad = d01 + jnp.where(inner_row, d23 + d45, 0.0)
    odd = pltpu.roll(q01, 32, 0)
    after = jnp.where(row < 31, pltpu.roll(q01, 63, 0), 0.0)
    quad = quad - 1.2 * jnp.where(row < 32, odd * (q01 + after), 0.0)
    quad = quad - 2.0 * jnp.where(last_row, 0.0, q23 * pltpu.roll(q23, 63, 0))
    quad = quad - 2.0 * jnp.where(inner_col & jnp.logical_not(last_row), q45 * pltpu.roll(q45, 63, 0), 0.0)
    quad = quad - jnp.where(low, s_low, s_high) * (e01 * (2.0 * q01 - e01))
    quad = quad - jnp.where(low, t_low, t_high) * (e23 * (2.0 * q23 - e23))
    await_halo(0)
    quad = quad - (2.0 * q01 + l01) * pair(hi_ref[0, 0], hi_ref[0, 1])
    quad = quad - 0.6 * (2.0 * q23 + l23) * pair(hj_ref[0, 0], hj_ref[0, 1])
    linear = corr[0] * image_vals[0]
    for f in range(1, 6):
        linear = linear + corr[f] * image_vals[f]
    total = jnp.sum(cacc + quad, keepdims=True) + 2.0 * jnp.sum(linear, keepdims=True)
    lanes = iota((1, 128), 1)
    corner = (lanes == 0) | (lanes == 127)
    corner = corner | (lanes == 63) | (lanes == 64)
    for at, (across, along) in enumerate(((e23[0:1], e45[0:1]), (e23[63:64], e45[63:64]),
                                          (e01[0:1], t45[0:1]), (e01[63:64], t45[63:64]))):
        cs_ref[2 * at : 2 * at + 1, :] = across + corners(along)
        rest = jnp.where(corner, 0.0, along)
        if at == 0:
            rest = jnp.where(lanes == 0, total, jnp.where(lanes == 127, gpart, rest))
        cs_ref[2 * at + 1 : 2 * at + 2, :] = rest
    cr_ref[me] = cs_ref[...]

    @peers
    def _(dd, dev):
        pltpu.make_async_remote_copy(src_ref=cs_ref, dst_ref=cr_ref.at[me], send_sem=c_s, recv_sem=c_r,
                                     device_id=dev, device_id_type=MESH).start()

    eh, el = split(e45)
    eh = jnp.concatenate([eh, el], axis=0)

    for c in range(T // CH):
        base = (c * (CH * 128))
        add = mm(eh, sel_ref[:, pl.ds(base, CH * 128)])
        for g in range(CH):
            at = ((c * CH + g) * 64)
            tile = add[:64, g * 128 : g * 128 + 128] + add[64:, g * 128 : g * 128 + 128]
            p_ref[pl.ds(at + 64, 64), :] = l_ref[pl.ds(at + 64, 64), :] + tile

    p_ref[64:128, :] += jnp.where(low64, e23, 0.0)
    p_ref[T * 64 : T * 64 + 64, :] += jnp.where(low64, 0.0, e23)
    top, bottom = e01[:32], e01[32:]
    edge0 = p_ref[pl.ds(64, 32, stride=64), :] + jnp.where(low32, top, swap(bottom))
    edge1 = p_ref[pl.ds(64 + 63, 32, stride=64), :] + jnp.where(low32, swap(top), bottom)
    p_ref[pl.ds(64, 32, stride=64), :] = edge0
    p_ref[pl.ds(64 + 63, 32, stride=64), :] = edge1

    p_ref[0:64, :] = jnp.zeros((64, 128), f32)
    p_ref[(T + 1) * 64 : (T + 2) * 64, :] = jnp.zeros((64, 128), f32)

    for q in range(T):
        value, _ = operate(p_ref, q)
        p_out[:, q * 128 : q * 128 + 128] = value
    send_halo(1, edge0, edge1, p_ref)
    await_halo(1)
    outside = 0.6 * pair(hj_ref[1, 0], hj_ref[1, 1])
    img_out[:, :128] = img_out[:, :128] - jnp.where(low64, outside, 0.0)
    img_out[:, (T - 1) * 128 :] = img_out[:, (T - 1) * 128 :] - jnp.where(low64, 0.0, outside)
    for q in range(T):
        at = slice(q * 128, q * 128 + 128)
        img_out[0:1, at] = img_out[0:1, at] - hi_ref[1, 0, q : q + 1, :]
        img_out[63:64, at] = img_out[63:64, at] - hi_ref[1, 1, q : q + 1, :]

    arrived(cr_ref, 8, c_r)
    both = cr_ref[0]
    first = jnp.zeros((8, 128), f32)
    second = jnp.zeros((8, 128), f32)
    for d in range(n):
        high = pltpu.roll(cr_ref[d], 6, 0)
        if d > 0:
            both = both + cr_ref[d]
        if d + ncg < n:
            first = first + high * cr_ref[d + ncg]
        if (d + 1) % ncg:
            second = second + high * cr_ref[d + 1]
    row8 = iota((8, 128), 0)
    lane8 = iota((8, 128), 1)
    cross = jnp.where(row8 < 2, first, jnp.where((row8 == 4) | (row8 == 5), 0.6 * second, 0.0))
    inside = ((lane8 & 63) > 0) & ((lane8 & 63) < 63)
    cross = jnp.where(inside | ((row8 & 1) == 0), -2.0 * cross, 0.0)
    curv = jnp.sum(cross, keepdims=True) + both[1:2, 0:1]
    gamma = both[1:2, 127:128]
    alpha_out[...] = gamma / curv

    arrived(ag_ref, 6, ag_s)
    arrived(a2r_ref, 6, a2_s)
    arrived(cr_ref, 8, c_s)
    for turn in range(2):
        for does, gets, dev, src, dst, a, b, k in sends:
            @pl.when(does)
            def _():
                halo(turn, dev, src, dst, a, b, k).wait_send()


def finish(p_ref, img_ref, x_ref, alpha_ref, sol_any, res_any, sol_ref, res_ref, sem):
    copies = []
    a = alpha_ref[...]
    for c in range(8):
        at = pl.ds(c * 8, 8)
        sol_ref[at, :] = a * p_ref[at, :]
        copies.append(pltpu.make_async_copy(sol_ref.at[at], sol_any.at[at], sem.at[0, c]))
        copies[-1].start()
        res_ref[at, :] = x_ref[at, :] - a * img_ref[at, :]
        copies.append(pltpu.make_async_copy(res_ref.at[at], res_any.at[at], sem.at[1, c]))
        copies[-1].start()
    for copy in copies:
        copy.wait()


def body(nsub, ncg, source, capacity, fd_weights, fd_modes, face_modes, coarse_map, fsai_cols, fsai_blocks):
    n = nsub * ncg
    nrow, nz = fsai_cols.shape
    vm = pl.BlockSpec(memory_space=pltpu.VMEM)
    hbm = pl.BlockSpec(memory_space=pltpu.HBM)
    field = jax.ShapeDtypeStruct(source.shape, f32)
    V = pltpu.VMEM
    dma = pltpu.SemaphoreType.DMA
    p, img, x, alpha = pl.pallas_call(
        functools.partial(kernel, nsub, ncg),
        out_shape=(field, field, field, jax.ShapeDtypeStruct((1, 1), f32)),
        in_specs=[hbm] * 8,
        out_specs=(vm, vm, vm, vm),
        scratch_shapes=[
            V(fd_modes.shape, f32),
            V((2, 64, 128), f32),
            V((6, 1, 128), jnp.int32),
            V(fsai_cols.shape, jnp.int32),
            V((T * 64, 128), f32),
            V((T * 64, 128), f32),
            V((64, T * 128), f32),
            V(((T + 2) * 64, 128), f32),
            V((64, T * 128), f32),
            V(fsai_blocks.shape, f32),
            V((128, T * 128), bf16),
            V((4, 64, 192), bf16),
            V((2, 256, 256), bf16),
            V((n, 8, 128), f32),
            V((8, 128), f32),
            V((n, 8, 128), f32),
            V((n, 8, 128), f32),
            V((nrow, nz, 128), f32),
            V((128 // nz, nz, 128), f32),
            V((2, 2, 32, 128), f32),
            V((2, 2, 32, 128), f32),
            V((2, 2, 32, 128), f32),
            V((2, 2, 32, 128), f32),
            V((8, 128), f32),
            V((n, 8, 128), f32),
            V(((T + 2) * 64, 128), f32),
            V((512, 128), f32),
            dma((8,)),
            dma, dma, dma, dma,
            dma((2, 4)), dma((2, 4)),
            dma, dma,
        ],
        compiler_params=pltpu.CompilerParams(collective_id=0, has_side_effects=True,
                                             vmem_limit_bytes=48 * 1024 * 1024),
        cost_estimate=pl.CostEstimate(flops=10**9, bytes_accessed=8 * 2**20, transcendentals=0),
        name="step",
    )(*(pltpu.with_memory_space_constraint(v, pltpu.HBM) for v in (
        source, fd_modes, jnp.swapaxes(face_modes, 1, 2), coarse_map.reshape(-1, 1, coarse_map.shape[-1]),
        fsai_cols, capacity, fd_weights, fsai_blocks)))
    return pl.pallas_call(
        finish,
        out_shape=(field, field),
        in_specs=[vm] * 4,
        out_specs=(hbm, hbm),
        scratch_shapes=[V(source.shape, f32), V(source.shape, f32), dma((2, 8))],
        cost_estimate=pl.CostEstimate(flops=2**20, bytes_accessed=2 * 2**20, transcendentals=0),
        name="finish",
    )(*(pltpu.with_memory_space_constraint(v, pltpu.VMEM) for v in (p, img, x, alpha)))


def solution(mesh):
    in_specs = (
        P("sub", "cgrp"),
        P("sub", "cgrp"),
        P("sub", "cgrp"),
        P(),
        P(),
        P("sub", "cgrp", None, None),
        P(("sub", "cgrp"), None),
        P(("sub", "cgrp"), None, None, None),
    )
    out_specs = (P("sub", "cgrp"), P("sub", "cgrp"))
    step = functools.partial(body, mesh.shape["sub"], mesh.shape["cgrp"])
    return jax.shard_map(step, mesh=mesh, in_specs=in_specs, out_specs=out_specs, check_vma=False)
```

```python
import functools
import jax
import jax.numpy as jnp
from jax import lax
from jax.experimental import pallas as pl
from jax.experimental.pallas import tpu as pltpu
from jax.sharding import PartitionSpec as P

C = 64
T = 32
CH = 8
f32 = jnp.float32
bf16 = jnp.bfloat16
HI = lax.Precision.HIGHEST
MESH = pl.DeviceIdType.MESH


def nn(a, b):
    return lax.dot_general(a, b, (((1,), (0,)), ((), ())), precision=HI, preferred_element_type=f32)


def nt(a, b):
    return lax.dot_general(a, b, (((1,), (1,)), ((), ())), precision=HI, preferred_element_type=f32)


def mm(a, b):
    return lax.dot_general(a, b, (((1,), (0,)), ((), ())), preferred_element_type=f32)


def mmt(a, b):
    return lax.dot_general(a, b, (((1,), (1,)), ((), ())), preferred_element_type=f32)


def split(x):
    hi = x.astype(bf16)
    return hi, (x - hi.astype(f32)).astype(bf16)


def iota(shape, dim):
    return lax.broadcasted_iota(jnp.int32, shape, dim)


def left3(m):
    hi, lo = split(m)
    return jnp.concatenate([hi, lo, hi], axis=1)


def rows3(x):
    hi, lo = split(x)
    return jnp.concatenate([hi, hi, lo], axis=0)


def lanes_weights(k):
    hi, lo = split(k)
    top = jnp.concatenate([hi, lo], axis=1)
    bottom = jnp.concatenate([hi, jnp.zeros_like(lo)], axis=1)
    return jnp.concatenate([top, bottom], axis=0)


def lane_transform(x, w):
    hi, lo = split(x)
    r = mm(jnp.concatenate([hi, lo], axis=1), w)
    return r[:, :128] + r[:, 128:]


def kernel(nsub, ncg, x_any, modes_any, face_any, map_any, cols_any, cap_any, wt_any, blk_any,
           p_out, img_out, x_ref, alpha_out,
           modes_ref, face_ref, map_ref, cols_ref,
           s_ref, z_ref, w_ref, p_ref, cap_ref, blk_ref, sel_ref, am_ref, kw_ref,
           ag_ref, send1_ref, a2s_ref, a2r_ref, pick_ref, spread_ref,
           hi_ref, his_ref, hj_ref, hjs_ref, cs_ref, cr_ref, l_ref, strip_ref,
           dsem, ag_s, ag_r, a2_s, a2_r, h_s, h_r, c_s, c_r):
    n = nsub * ncg
    s = lax.axis_index("sub")
    t = lax.axis_index("cgrp")
    me = s * ncg + t

    def peer(o):
        d = lax.rem(me + o, n)
        return d, (lax.div(d, ncg), lax.rem(d, ncg))

    early = [pltpu.make_async_copy(src, dst, dsem.at[k]) for k, (src, dst) in enumerate((
        (face_any, face_ref), (map_any, map_ref), (x_any, x_ref), (modes_any, modes_ref), (cols_any, cols_ref),
        (wt_any, w_ref), (blk_any, blk_ref), (cap_any, cap_ref)))]
    for copy in early[:5]:
        copy.start()
    fcopy, mcopy, xcopy, ocopy, lcopy, wcopy, bcopy, ccopy = early

    def mirror(v, bits):
        out = v
        for k in range(8):
            if bits >> k & 1:
                out = out + (1 << k) - (2 << k) * lax.rem(lax.div(v, 1 << k), 2)
        return out

    def peers(step):
        if n > 32:
            @pl.loop(1, n)
            def _(o):
                step(*peer(o))
        else:
            pairs = [(a, b) for a in range(nsub) for b in range(ncg) if a or b]
            for a, b in sorted(pairs, key=lambda ab: -(ab[0] + (ab[1] >> 1 & 1) + (ab[1] >> 2 & 1))):
                ds, dt = mirror(s, a), mirror(t, b)
                step(ds * ncg + dt, (ds, dt))

    def arrived(ref, rows, sem):
        part = ref.at[pl.ds(0, n - 1), pl.ds(0, rows)]
        pltpu.make_async_copy(part, part, sem).wait()

    ag_ref[...] = jnp.zeros_like(ag_ref)
    a2r_ref[...] = jnp.zeros_like(a2r_ref)
    barrier = pltpu.get_barrier_semaphore()

    @pl.loop(1, n)
    def _(o):
        _, dev = peer(o)
        pl.semaphore_signal(barrier, inc=1, device_id=dev, device_id_type=MESH)

    lane = iota((1, 128), 1)
    low = lane < 64
    low32 = jnp.broadcast_to(low, (32, 128))
    low64 = jnp.broadcast_to(low, (64, 128))

    def swap(a):
        return pltpu.roll(a, 64, 1)

    @pl.loop(0, 8)
    def _(c):
        r = iota((128, 512), 0)
        col = iota((128, 512), 1) + c * 512
        hit = ((col >> 6) == (r & 63)) & ((col & 63) == 63 * (r >> 6))
        sel_ref[:, pl.ds(pl.multiple_of(c * 512, 512), 512)] = jnp.where(hit, 1.0, 0.0).astype(bf16)

    fcopy.wait()
    mcopy.wait()
    fm0t = face_ref[0]
    fm1t = face_ref[1]
    r64 = iota((64, 64), 0)
    c64 = iota((64, 64), 1)
    eye64 = jnp.where(r64 == c64, 1.0, 0.0)
    qm = jnp.where(c64 == 2 * (r64 & 31) + (r64 >> 5), 1.0, 0.0)
    dup = jnp.where((iota((64, 128), 1) & 63) == iota((64, 128), 0), 1.0, 0.0)
    dupt = jnp.where((iota((128, 64), 0) & 63) == iota((128, 64), 1), 1.0, 0.0)
    eye128 = jnp.where(iota((128, 128), 0) == iota((128, 128), 1), 1.0, 0.0)
    fm0pt = nn(qm, fm0t)

    mapf = [(map_ref[f] & 127).astype(f32) for f in range(6)]
    mapf = jnp.concatenate(mapf + [jnp.zeros((2, 128), f32)], axis=0)
    mapt = mmt(eye128.astype(bf16), mapf.astype(bf16))
    lanef = iota((128, 128), 1).astype(f32)
    hot = [jnp.where(mapt[:, f : f + 1] == lanef, 1.0, 0.0).astype(bf16) for f in range(6)]

    def in_order(mats, faces):
        m = jnp.concatenate(mats, axis=0)
        hi, lo = split(m)
        rest = (m - hi.astype(f32) - lo.astype(f32)).astype(bf16)
        size = m.shape[0]
        r = mm(jnp.concatenate([hi, lo, rest], axis=0), jnp.concatenate([hot[f] for f in faces], axis=1))
        r = r[:size] + r[size : 2 * size] + r[2 * size :]
        return [r[k * 64 : k * 64 + 64] for k in range(len(mats))]

    def apart(m):
        zero = jnp.zeros((64, 128), f32)
        return jnp.concatenate([jnp.concatenate([m[:, :128], zero], axis=1),
                                jnp.concatenate([zero, m[:, 128:]], axis=1)], axis=0)

    a01, b01 = in_order([fm0pt, fm1t], (0, 1))
    a25, b25 = in_order([fm0t, fm1t], (2, 3, 4, 5))
    a23, a45, b23, b45 = a25[:, :256], a25[:, 256:], b25[:, :256], b25[:, 256:]
    w01, w23, w45 = apart(b01), apart(b23), apart(b45)
    w01r, w23r, w45r = rows3(w01), rows3(w23), rows3(w45)

    xcopy.wait()
    for copy in early[5:]:
        copy.start()

    def pair(a, b):
        return jnp.concatenate([jnp.where(low32, a, swap(b)), jnp.where(low32, swap(a), b)], axis=0)

    def planes(ref):
        for q in range(T):
            strip_ref[q * 8 : q * 8 + 8, :] = ref[0:8, q * 128 : q * 128 + 128]
            strip_ref[256 + q * 8 : 256 + q * 8 + 8, :] = ref[56:64, q * 128 : q * 128 + 128]
        y0 = strip_ref[pl.ds(0, 32, stride=8), :]
        y1 = strip_ref[pl.ds(263, 32, stride=8), :]
        f01 = pair(y0, y1)
        f23 = jnp.where(low64, ref[:, :128], ref[:, 31 * 128 :])
        f45 = mmt(jnp.concatenate(split(ref[...]), axis=0), sel_ref[...])
        return f01, f23, f45[:64] + f45[64:]

    def restrict(f01, f23, f45):
        return [jnp.sum(mm(left3(plane), w) * a, axis=0, keepdims=True)
                for plane, w, a in ((f01, w01r, a01), (f23, w23r, a23), (f45, w45r, a45))]

    rows = []
    for both in restrict(*planes(x_ref)):
        rows.extend([both[:, :128], both[:, 128:]])
    mine = jnp.concatenate(rows + [jnp.zeros((2, 128), f32)], axis=0)
    send1_ref[...] = mine
    ag_ref[me] = mine

    pl.semaphore_wait(barrier, n - 1)

    @peers
    def _(dd, dev):
        pltpu.make_async_remote_copy(src_ref=send1_ref.at[pl.ds(0, 6)], dst_ref=ag_ref.at[me, pl.ds(0, 6)],
                                     send_sem=ag_s, recv_sem=ag_r,
                                     device_id=dev, device_id_type=MESH).start()

    ocopy.wait()
    m0, m1, m2 = modes_ref[0], modes_ref[1], modes_ref[2]
    am_ref[0] = left3(m0)
    am_ref[1] = left3(nt(eye64, m0))
    am_ref[2] = left3(nt(nn(qm, m1), qm))
    am_ref[3] = left3(nt(nt(qm, m1), qm))
    block = (iota((128, 128), 0) >> 6) == (iota((128, 128), 1) >> 6)
    kw_ref[0] = lanes_weights(jnp.where(block, nn(nt(dupt, m2), dup), 0.0))
    kw_ref[1] = lanes_weights(jnp.where(block, nn(dupt, nn(m2, dup)), 0.0))

    for c in range(T // CH):
        base = (c * (CH * 128))
        y = mm(am_ref[0], rows3(x_ref[:, pl.ds(base, CH * 128)]))
        stacked = jnp.concatenate([y[:, g * 128 : g * 128 + 128] for g in range(CH)], axis=0)
        s_ref[pl.ds((c * (CH * 64)), CH * 64), :] = lane_transform(stacked, kw_ref[0])

    wcopy.wait()
    for q in range(T):
        z_ref[q * 64 : q * 64 + 64, :] = w_ref[:, q * 128 : q * 128 + 128]

    def turned(ref, u):
        a = ref[pl.ds(u, 32, stride=64), :]
        b = ref[pl.ds(u + 32, 32, stride=64), :]
        return jnp.concatenate([jnp.where(low32, a, swap(b)), jnp.where(low32, swap(a), b)], axis=0)

    def middle(c, acc):
        fwd = jnp.concatenate([turned(s_ref, c * CH + g) for g in range(CH)], axis=1)
        wts = jnp.concatenate([turned(z_ref, c * CH + g) for g in range(CH)], axis=1)
        v = mm(am_ref[2], rows3(fwd))
        wv = wts * v
        prod = wv * v
        for g in range(CH):
            acc = acc + prod[:, g * 128 : g * 128 + 128]
        y = mm(am_ref[3], rows3(wv))
        for g in range(CH):
            p_ref[pl.ds((64 + (c * CH + g) * 64), 64), :] = y[:, g * 128 : g * 128 + 128]
        return acc

    gacc = jnp.zeros((64, 128), f32)
    for c in range(T // CH):
        gacc = middle(c, gacc)

    ccopy.wait()
    cap01, cap23, cap45 = planes(cap_ref)

    lcopy.wait()
    cols = cols_ref[...]
    nrow = cols.shape[0]
    nz = cols.shape[1]
    wide_cols = jnp.concatenate([jnp.broadcast_to(cols[i : i + 1, :], (nz, nz)) for i in range(nrow)], axis=0)
    kk = nrow * nz
    pick_diag = iota((kk, nz), 1) == (iota((kk, nz), 0) & (nz - 1))
    colv = jnp.sum(jnp.where(pick_diag, wide_cols.astype(f32), 0.0), axis=1, keepdims=True)
    r = iota((1, n * 8), 1)
    d = r >> 3
    f = r & 7
    own = nrow * d + f
    own = jnp.where((f == 0) & (d >= ncg), nrow * (d - ncg) + 1, own)
    own = jnp.where((f == 2) & (lax.rem(d, ncg) > 0), nrow * (d - 1) + 3, own)
    own = jnp.where(f >= 6, -1, own).astype(f32)
    g1 = jnp.where(colv == own, 1.0, 0.0)
    g1 = jnp.concatenate([g1, jnp.zeros((128 - kk, n * 8), f32)], axis=0)

    g2 = g1.T.astype(bf16)
    g2 = jnp.concatenate([g2, g2], axis=1)
    g1 = g1.astype(bf16)

    arrived(ag_ref, 6, ag_r)
    th, tl = split(ag_ref[...].reshape(n * 8, 128))
    picked = mm(g1, th) + mm(g1, tl)
    pick_ref[...] = picked[:kk].reshape(nrow, nz, 128)
    bcopy.wait()
    spread_ref[...] = jnp.zeros_like(spread_ref)

    def coarse_row(i, acc):
        pk = pick_ref[i]
        tot = blk_ref[i, 0] * pk[0:1]
        for k in range(1, nz):
            tot = tot + blk_ref[i, k] * pk[k : k + 1]
        img = jnp.sum(tot, axis=1, keepdims=True)
        out = [jnp.sum(blk_ref[i, k] * img, axis=0, keepdims=True) for k in range(nz)]
        spread_ref[i] = jnp.concatenate(out, axis=0)
        return acc + img * img

    iacc = jnp.zeros((128, 1), f32)
    for i in range(nrow):
        iacc = coarse_row(i, iacc)
    back = mm(g2, jnp.concatenate(split(spread_ref[...].reshape(128, 128)), axis=0))
    a2s_ref[...] = back.reshape(n, 8, 128)
    a2r_ref[me] = a2s_ref[me]

    @peers
    def _(dd, dev):
        pltpu.make_async_remote_copy(src_ref=a2s_ref.at[dd, pl.ds(0, 6)], dst_ref=a2r_ref.at[me, pl.ds(0, 6)],
                                     send_sem=a2_s, recv_sem=a2_r,
                                     device_id=dev, device_id_type=MESH).start()

    gpart = jnp.sum(iacc, keepdims=True) + jnp.sum(gacc, keepdims=True)

    for c in range(T // CH):
        tiles = []
        for g in range(CH):
            a = p_ref[pl.ds(64 + c * CH + g, 32, stride=64), :]
            b = p_ref[pl.ds(96 + c * CH + g, 32, stride=64), :]
            tiles.append(jnp.where(low32, a, swap(b)))
            tiles.append(jnp.where(low32, swap(a), b))
        k = lane_transform(jnp.concatenate(tiles, axis=0), kw_ref[1])
        y = jnp.concatenate([k[g * 64 : g * 64 + 64] for g in range(CH)], axis=1)
        y = mm(am_ref[1], rows3(y))
        for g in range(CH):
            l_ref[pl.ds(((c * CH + g) * 64 + 64), 64), :] = y[:, g * 128 : g * 128 + 128]

    row = iota((64, 128), 0)
    kpos = iota((64, 128), 1) & 63

    def operate(ref, q):
        at = q * 64
        x = ref[pl.ds(at + 64, 64), :]
        second = swap(x + jnp.where(low64, ref[pl.ds(at + 128, 64), :], ref[pl.ds(at, 64), :]))
        up = jnp.where(row == 0, 0.0, pltpu.roll(x, 1, 0))
        down = jnp.where(row == 63, 0.0, pltpu.roll(x, 63, 0))
        third = jnp.where(kpos == 0, 0.0, pltpu.roll(x, 1, 1)) + jnp.where(kpos == 63, 0.0, pltpu.roll(x, 127, 1))
        cols_at = pl.ds(q * 128, 128)
        img = (cap_ref[:, cols_at] + 8.2) * x - (up + down) - 0.6 * second - 2.5 * third
        img_out[:, cols_at] = img
        return x, img

    sends = (
        (s > 0, s < nsub - 1, (s - 1, t), his_ref, hi_ref, 0, 1, 0),
        (s < nsub - 1, s > 0, (s + 1, t), his_ref, hi_ref, 1, 0, 1),
        (t > 0, t < ncg - 1, (s, t - 1), hjs_ref, hj_ref, 0, 1, 2),
        (t < ncg - 1, t > 0, (s, t + 1), hjs_ref, hj_ref, 1, 0, 3),
    )

    def halo(turn, dev, src, dst, a, b, k):
        return pltpu.make_async_remote_copy(src_ref=src.at[turn, a], dst_ref=dst.at[turn, b], send_sem=h_s.at[turn, k],
                                            recv_sem=h_r.at[turn, k], device_id=dev, device_id_type=MESH)

    def send_halo(turn, edge0, edge1, ref):
        his_ref[turn, 0] = edge0
        his_ref[turn, 1] = edge1
        hjs_ref[turn, 0] = jnp.where(low32, ref[64:96, :], swap(ref[96:128, :]))
        hjs_ref[turn, 1] = jnp.where(low32, swap(ref[T * 64 : T * 64 + 32, :]), ref[T * 64 + 32 : T * 64 + 64, :])
        for does, gets, dev, src, dst, a, b, k in sends:
            @pl.when(does)
            def _():
                halo(turn, dev, src, dst, a, b, k).start()

            @pl.when(jnp.logical_not(gets))
            def _():
                dst[turn, b] = jnp.zeros(dst.shape[2:], f32)

    def await_halo(turn):
        for does, gets, dev, src, dst, a, b, k in sends:
            @pl.when(gets)
            def _():
                halo(turn, dev, src, dst, a, b, k).wait_recv()

    l_ref[0:64, :] = jnp.zeros((64, 128), f32)
    l_ref[(T + 1) * 64 : (T + 2) * 64, :] = jnp.zeros((64, 128), f32)
    ledge0 = l_ref[pl.ds(64, 32, stride=64), :]
    ledge1 = l_ref[pl.ds(64 + 63, 32, stride=64), :]
    send_halo(0, ledge0, ledge1, l_ref)
    cacc = jnp.zeros((64, 128), f32)
    for q in range(T):
        value, img = operate(l_ref, q)
        cacc = cacc + value * img
    l01 = pair(ledge0, ledge1)
    l23 = jnp.where(low64, l_ref[64:128, :], l_ref[T * 64 : T * 64 + 64, :])
    image_vals = restrict(*planes(img_out))

    (n01,) = in_order([fm0t], (0, 1))
    (p45,) = in_order([nn(qm, fm1t)], (4, 5))
    ends01 = jnp.concatenate([b01[0:8], b01[56:64]], axis=0)
    x01, x23, x45 = rows3(w01.T), rows3(w23.T), rows3(w45.T)
    y01, y45 = rows3(apart(n01).T), rows3(apart(a45).T)
    inner_row = (row > 0) & (row < 63)
    inner_col = (kpos > 0) & (kpos < 63)
    last_row = row == 63
    last_col = kpos == 63
    s_low = jnp.where(s > 0, 1.0, 0.0)
    s_high = jnp.where(s < nsub - 1, 1.0, 0.0)
    t_low = jnp.where(t > 0, 0.6, 0.0)
    t_high = jnp.where(t < ncg - 1, 0.6, 0.0)

    arrived(a2r_ref, 6, a2_r)
    backs = jnp.sum(a2r_ref[...], axis=0)
    v01, v23, v45 = (jnp.concatenate([backs[f : f + 1], backs[f + 1 : f + 2]], axis=1) for f in (0, 2, 4))
    e01 = mm(left3(a01 * v01), x01)
    e23 = mm(left3(a23 * v23), x23)
    e45 = mm(left3(a45 * v45), x45)
    t01 = mm(left3(ends01 * v01), y01)
    t45 = mm(left3(p45 * v45), y45)

    def corners(e):
        lanes = iota(e.shape, 1)
        ends = jnp.where((lanes == 0) | (lanes == 127), e, 0.0)
        ends = jnp.where(lanes == 63, pltpu.roll(e, 127, 1), ends)
        return jnp.where(lanes == 64, pltpu.roll(e, 1, 1), ends)

    def whole(e, side, first, last):
        ends = jnp.where(row == 0, jnp.where(low, first, swap(last)), 0.0)
        ends = jnp.where(row == 63, jnp.where(low, swap(first), last), ends)
        return e + corners(side) + ends

    q01 = whole(e01, t45, e23[0:1], e23[63:64])
    q23 = whole(e23, e45, e01[0:1], e01[63:64])
    q45 = whole(e45, e23, t01[0:1], t01[15:16])
    k01, k23, k45 = (jnp.where(last_col, 0.0, pltpu.roll(v, 127, 1)) for v in (q01, q23, q45))
    d01 = q01 * ((cap01 + 8.2) * q01 - 5.0 * k01)
    d23 = q23 * ((cap23 + 8.2) * q23 - 5.0 * k23)
    d45 = q45 * (jnp.where(inner_col, (cap45 + 8.2) * q45, 0.0) - 1.2 * k45)
    quad = d01 + jnp.where(inner_row, d23 + d45, 0.0)
    odd = pltpu.roll(q01, 32, 0)
    after = jnp.where(row < 31, pltpu.roll(q01, 63, 0), 0.0)
    quad = quad - 1.2 * jnp.where(row < 32, odd * (q01 + after), 0.0)
    quad = quad - 2.0 * jnp.where(last_row, 0.0, q23 * pltpu.roll(q23, 63, 0))
    quad = quad - 2.0 * jnp.where(inner_col & jnp.logical_not(last_row), q45 * pltpu.roll(q45, 63, 0), 0.0)
    quad = quad - jnp.where(low, s_low, s_high) * (e01 * (2.0 * q01 - e01))
    quad = quad - jnp.where(low, t_low, t_high) * (e23 * (2.0 * q23 - e23))
    await_halo(0)
    quad = quad - (2.0 * q01 + l01) * pair(hi_ref[0, 0], hi_ref[0, 1])
    quad = quad - 0.6 * (2.0 * q23 + l23) * pair(hj_ref[0, 0], hj_ref[0, 1])
    linear = v01 * image_vals[0] + v23 * image_vals[1] + v45 * image_vals[2]
    total = jnp.sum(cacc + quad, keepdims=True) + 2.0 * jnp.sum(linear, keepdims=True)
    lanes = iota((1, 128), 1)
    corner = (lanes == 0) | (lanes == 127)
    corner = corner | (lanes == 63) | (lanes == 64)
    for at, (across, along) in enumerate(((e23[0:1], e45[0:1]), (e23[63:64], e45[63:64]),
                                          (e01[0:1], t45[0:1]), (e01[63:64], t45[63:64]))):
        cs_ref[2 * at : 2 * at + 1, :] = across + corners(along)
        rest = jnp.where(corner, 0.0, along)
        if at == 0:
            rest = jnp.where(lanes == 0, total, jnp.where(lanes == 127, gpart, rest))
        cs_ref[2 * at + 1 : 2 * at + 2, :] = rest
    cr_ref[me] = cs_ref[...]

    @peers
    def _(dd, dev):
        pltpu.make_async_remote_copy(src_ref=cs_ref, dst_ref=cr_ref.at[me], send_sem=c_s, recv_sem=c_r,
                                     device_id=dev, device_id_type=MESH).start()

    eh, el = split(e45)
    eh = jnp.concatenate([eh, el], axis=0)

    for c in range(T // CH):
        base = (c * (CH * 128))
        add = mm(eh, sel_ref[:, pl.ds(base, CH * 128)])
        for g in range(CH):
            at = ((c * CH + g) * 64)
            tile = add[:64, g * 128 : g * 128 + 128] + add[64:, g * 128 : g * 128 + 128]
            p_ref[pl.ds(at + 64, 64), :] = l_ref[pl.ds(at + 64, 64), :] + tile

    p_ref[64:128, :] += jnp.where(low64, e23, 0.0)
    p_ref[T * 64 : T * 64 + 64, :] += jnp.where(low64, 0.0, e23)
    top, bottom = e01[:32], e01[32:]
    edge0 = p_ref[pl.ds(64, 32, stride=64), :] + jnp.where(low32, top, swap(bottom))
    edge1 = p_ref[pl.ds(64 + 63, 32, stride=64), :] + jnp.where(low32, swap(top), bottom)
    p_ref[pl.ds(64, 32, stride=64), :] = edge0
    p_ref[pl.ds(64 + 63, 32, stride=64), :] = edge1

    p_ref[0:64, :] = jnp.zeros((64, 128), f32)
    p_ref[(T + 1) * 64 : (T + 2) * 64, :] = jnp.zeros((64, 128), f32)

    for q in range(T):
        value, _ = operate(p_ref, q)
        p_out[:, q * 128 : q * 128 + 128] = value
    send_halo(1, edge0, edge1, p_ref)
    await_halo(1)
    outside = 0.6 * pair(hj_ref[1, 0], hj_ref[1, 1])
    img_out[:, :128] = img_out[:, :128] - jnp.where(low64, outside, 0.0)
    img_out[:, (T - 1) * 128 :] = img_out[:, (T - 1) * 128 :] - jnp.where(low64, 0.0, outside)
    for q in range(T):
        at = slice(q * 128, q * 128 + 128)
        img_out[0:1, at] = img_out[0:1, at] - hi_ref[1, 0, q : q + 1, :]
        img_out[63:64, at] = img_out[63:64, at] - hi_ref[1, 1, q : q + 1, :]

    arrived(cr_ref, 8, c_r)
    both = cr_ref[0]
    first = jnp.zeros((8, 128), f32)
    second = jnp.zeros((8, 128), f32)
    for d in range(n):
        high = pltpu.roll(cr_ref[d], 6, 0)
        if d > 0:
            both = both + cr_ref[d]
        if d + ncg < n:
            first = first + high * cr_ref[d + ncg]
        if (d + 1) % ncg:
            second = second + high * cr_ref[d + 1]
    row8 = iota((8, 128), 0)
    lane8 = iota((8, 128), 1)
    cross = jnp.where(row8 < 2, first, jnp.where((row8 == 4) | (row8 == 5), 0.6 * second, 0.0))
    inside = ((lane8 & 63) > 0) & ((lane8 & 63) < 63)
    cross = jnp.where(inside | ((row8 & 1) == 0), -2.0 * cross, 0.0)
    curv = jnp.sum(cross, keepdims=True) + both[1:2, 0:1]
    gamma = both[1:2, 127:128]
    alpha_out[...] = gamma / curv

    arrived(ag_ref, 6, ag_s)
    arrived(a2r_ref, 6, a2_s)
    arrived(cr_ref, 8, c_s)
    for turn in range(2):
        for does, gets, dev, src, dst, a, b, k in sends:
            @pl.when(does)
            def _():
                halo(turn, dev, src, dst, a, b, k).wait_send()


def finish(p_ref, img_ref, x_ref, alpha_ref, sol_any, res_any, sol_ref, res_ref, sem):
    a = alpha_ref[...]
    for c in range(4):
        at = pl.ds(c * 16, 16)
        sol_ref[at, :] = a * p_ref[at, :]
        pltpu.make_async_copy(sol_ref.at[at], sol_any.at[at], sem.at[0]).start()
        res_ref[at, :] = x_ref[at, :] - a * img_ref[at, :]
        pltpu.make_async_copy(res_ref.at[at], res_any.at[at], sem.at[1]).start()
    pltpu.make_async_copy(sol_ref, sol_any, sem.at[0]).wait()
    pltpu.make_async_copy(res_ref, res_any, sem.at[1]).wait()


def body(nsub, ncg, source, capacity, fd_weights, fd_modes, face_modes, coarse_map, fsai_cols, fsai_blocks):
    n = nsub * ncg
    nrow, nz = fsai_cols.shape
    vm = pl.BlockSpec(memory_space=pltpu.VMEM)
    hbm = pl.BlockSpec(memory_space=pltpu.HBM)
    field = jax.ShapeDtypeStruct(source.shape, f32)
    V = pltpu.VMEM
    dma = pltpu.SemaphoreType.DMA
    p, img, x, alpha = pl.pallas_call(
        functools.partial(kernel, nsub, ncg),
        out_shape=(field, field, field, jax.ShapeDtypeStruct((1, 1), f32)),
        in_specs=[hbm] * 8,
        out_specs=(vm, vm, vm, vm),
        scratch_shapes=[
            V(fd_modes.shape, f32),
            V((2, 64, 128), f32),
            V((6, 1, 128), jnp.int32),
            V(fsai_cols.shape, jnp.int32),
            V((T * 64, 128), f32),
            V((T * 64, 128), f32),
            V((64, T * 128), f32),
            V(((T + 2) * 64, 128), f32),
            V((64, T * 128), f32),
            V(fsai_blocks.shape, f32),
            V((128, T * 128), bf16),
            V((4, 64, 192), bf16),
            V((2, 256, 256), bf16),
            V((n, 8, 128), f32),
            V((8, 128), f32),
            V((n, 8, 128), f32),
            V((n, 8, 128), f32),
            V((nrow, nz, 128), f32),
            V((128 // nz, nz, 128), f32),
            V((2, 2, 32, 128), f32),
            V((2, 2, 32, 128), f32),
            V((2, 2, 32, 128), f32),
            V((2, 2, 32, 128), f32),
            V((8, 128), f32),
            V((n, 8, 128), f32),
            V(((T + 2) * 64, 128), f32),
            V((512, 128), f32),
            dma((8,)),
            dma, dma, dma, dma,
            dma((2, 4)), dma((2, 4)),
            dma, dma,
        ],
        compiler_params=pltpu.CompilerParams(collective_id=0, has_side_effects=True,
                                             vmem_limit_bytes=48 * 1024 * 1024),
        cost_estimate=pl.CostEstimate(flops=10**9, bytes_accessed=8 * 2**20, transcendentals=0),
        name="step",
    )(*(pltpu.with_memory_space_constraint(v, pltpu.HBM) for v in (
        source, fd_modes, jnp.swapaxes(face_modes, 1, 2), coarse_map.reshape(-1, 1, coarse_map.shape[-1]),
        fsai_cols, capacity, fd_weights, fsai_blocks)))
    return pl.pallas_call(
        finish,
        out_shape=(field, field),
        in_specs=[vm] * 4,
        out_specs=(hbm, hbm),
        scratch_shapes=[V(source.shape, f32), V(source.shape, f32), dma((2,))],
        cost_estimate=pl.CostEstimate(flops=2**20, bytes_accessed=2 * 2**20, transcendentals=0),
        name="finish",
    )(*(pltpu.with_memory_space_constraint(v, pltpu.VMEM) for v in (p, img, x, alpha)))


def solution(mesh):
    in_specs = (
        P("sub", "cgrp"),
        P("sub", "cgrp"),
        P("sub", "cgrp"),
        P(),
        P(),
        P("sub", "cgrp", None, None),
        P(("sub", "cgrp"), None),
        P(("sub", "cgrp"), None, None, None),
    )
    out_specs = (P("sub", "cgrp"), P("sub", "cgrp"))
    step = functools.partial(body, mesh.shape["sub"], mesh.shape["cgrp"])
    return jax.shard_map(step, mesh=mesh, in_specs=in_specs, out_specs=out_specs, check_vma=False)
```

```python
import functools
import jax
import jax.numpy as jnp
from jax import lax
from jax.experimental import pallas as pl
from jax.experimental.pallas import tpu as pltpu
from jax.sharding import PartitionSpec as P

C = 64
T = 32
CH = 8
f32 = jnp.float32
bf16 = jnp.bfloat16
HI = lax.Precision.HIGHEST
MESH = pl.DeviceIdType.MESH


def nn(a, b):
    return lax.dot_general(a, b, (((1,), (0,)), ((), ())), precision=HI, preferred_element_type=f32)


def nt(a, b):
    return lax.dot_general(a, b, (((1,), (1,)), ((), ())), precision=HI, preferred_element_type=f32)


def mm(a, b):
    return lax.dot_general(a, b, (((1,), (0,)), ((), ())), preferred_element_type=f32)


def mmt(a, b):
    return lax.dot_general(a, b, (((1,), (1,)), ((), ())), preferred_element_type=f32)


def split(x):
    hi = x.astype(bf16)
    return hi, (x - hi.astype(f32)).astype(bf16)


def iota(shape, dim):
    return lax.broadcasted_iota(jnp.int32, shape, dim)


def left3(m):
    hi, lo = split(m)
    return jnp.concatenate([hi, lo, hi], axis=1)


def rows3(x):
    hi, lo = split(x)
    return jnp.concatenate([hi, hi, lo], axis=0)


def lanes_weights(k):
    hi, lo = split(k)
    top = jnp.concatenate([hi, lo], axis=1)
    bottom = jnp.concatenate([hi, jnp.zeros_like(lo)], axis=1)
    return jnp.concatenate([top, bottom], axis=0)


def lane_transform(x, w):
    hi, lo = split(x)
    r = mm(jnp.concatenate([hi, lo], axis=1), w)
    return r[:, :128] + r[:, 128:]


def kernel(nsub, ncg, x_any, modes_any, face_any, map_any, cols_any, cap_any, wt_any, blk_any,
           p_out, img_out, x_ref, alpha_out,
           modes_ref, face_ref, map_ref, cols_ref,
           s_ref, z_ref, w_ref, p_ref, cap_ref, blk_ref, sel_ref, am_ref, kw_ref,
           ag_ref, send1_ref, a2s_ref, a2r_ref,
           hi_ref, his_ref, hj_ref, hjs_ref, cs_ref, cr_ref, l_ref, strip_ref,
           dsem, out_s, ag_r, a2_r, h_r, c_r):
    n = nsub * ncg
    s = lax.axis_index("sub")
    t = lax.axis_index("cgrp")
    me = s * ncg + t

    def peer(o):
        d = lax.rem(me + o, n)
        return d, (lax.div(d, ncg), lax.rem(d, ncg))

    early = [pltpu.make_async_copy(src, dst, dsem.at[k]) for k, (src, dst) in enumerate((
        (face_any, face_ref), (map_any, map_ref), (x_any, x_ref), (modes_any, modes_ref), (cols_any, cols_ref),
        (wt_any, w_ref), (blk_any, blk_ref), (cap_any, cap_ref)))]
    for copy in early[:5]:
        copy.start()
    fcopy, mcopy, xcopy, ocopy, lcopy, wcopy, bcopy, ccopy = early

    def mirrors(v, size):
        out = [v]
        while len(out) < size:
            bit = len(out)
            flip = bit - 2 * bit * lax.rem(lax.div(v, bit), 2)
            out = out + [o + flip for o in out]
        return out

    if n <= 32:
        to_s, to_t = mirrors(s, nsub), mirrors(t, ncg)
        order = [(a, b) for a in range(nsub) for b in range(ncg) if a or b]
        order.sort(key=lambda ab: -(min(ab[0], 2) + (ab[1] >> 1 & 1) + (ab[1] >> 2 & 1)))

    def peers(step):
        if n > 32:
            @pl.loop(1, n)
            def _(o):
                step(*peer(o))
        else:
            for a, b in order:
                step(to_s[a] * ncg + to_t[b], (to_s[a], to_t[b]))

    def arrived(ref, rows, sem):
        part = ref.at[pl.ds(0, n - 1), pl.ds(0, rows)]
        pltpu.make_async_copy(part, part, sem).wait()

    ag_ref[...] = jnp.zeros_like(ag_ref)
    a2r_ref[...] = jnp.zeros_like(a2r_ref)
    barrier = pltpu.get_barrier_semaphore()

    @pl.loop(1, n)
    def _(o):
        _, dev = peer(o)
        pl.semaphore_signal(barrier, inc=1, device_id=dev, device_id_type=MESH)

    lane = iota((1, 128), 1)
    low = lane < 64
    low32 = jnp.broadcast_to(low, (32, 128))
    low64 = jnp.broadcast_to(low, (64, 128))

    def swap(a):
        return pltpu.roll(a, 64, 1)

    @pl.loop(0, 8)
    def _(c):
        r = iota((128, 512), 0)
        col = iota((128, 512), 1) + c * 512
        hit = ((col >> 6) == (r & 63)) & ((col & 63) == 63 * (r >> 6))
        sel_ref[:, pl.ds(pl.multiple_of(c * 512, 512), 512)] = jnp.where(hit, 1.0, 0.0).astype(bf16)

    fcopy.wait()
    mcopy.wait()
    fm0t = face_ref[0]
    fm1t = face_ref[1]
    r64 = iota((64, 64), 0)
    c64 = iota((64, 64), 1)
    eye64 = jnp.where(r64 == c64, 1.0, 0.0)
    qm = jnp.where(c64 == 2 * (r64 & 31) + (r64 >> 5), 1.0, 0.0)
    dup = jnp.where((iota((64, 128), 1) & 63) == iota((64, 128), 0), 1.0, 0.0)
    dupt = jnp.where((iota((128, 64), 0) & 63) == iota((128, 64), 1), 1.0, 0.0)
    eye128 = jnp.where(iota((128, 128), 0) == iota((128, 128), 1), 1.0, 0.0)
    fm0pt = nn(qm, fm0t)

    mapf = [(map_ref[f] & 127).astype(f32) for f in range(6)]
    mapf = jnp.concatenate(mapf + [jnp.zeros((2, 128), f32)], axis=0)
    mapt = mmt(eye128.astype(bf16), mapf.astype(bf16))
    lanef = iota((128, 128), 1).astype(f32)
    hot = [jnp.where(mapt[:, f : f + 1] == lanef, 1.0, 0.0).astype(bf16) for f in range(6)]

    def in_order(mats, faces):
        m = jnp.concatenate(mats, axis=0)
        hi, lo = split(m)
        rest = (m - hi.astype(f32) - lo.astype(f32)).astype(bf16)
        size = m.shape[0]
        r = mm(jnp.concatenate([hi, lo, rest], axis=0), jnp.concatenate([hot[f] for f in faces], axis=1))
        r = r[:size] + r[size : 2 * size] + r[2 * size :]
        return [r[k * 64 : k * 64 + 64] for k in range(len(mats))]

    def apart(m):
        zero = jnp.zeros((64, 128), f32)
        return jnp.concatenate([jnp.concatenate([m[:, :128], zero], axis=1),
                                jnp.concatenate([zero, m[:, 128:]], axis=1)], axis=0)

    a01, b01 = in_order([fm0pt, fm1t], (0, 1))
    a25, b25 = in_order([fm0t, fm1t], (2, 3, 4, 5))
    a23, a45, b23, b45 = a25[:, :256], a25[:, 256:], b25[:, :256], b25[:, 256:]
    w01, w23, w45 = apart(b01), apart(b23), apart(b45)
    w01r, w23r, w45r = rows3(w01), rows3(w23), rows3(w45)

    xcopy.wait()
    for copy in early[5:]:
        copy.start()

    def pair(a, b):
        return jnp.concatenate([jnp.where(low32, a, swap(b)), jnp.where(low32, swap(a), b)], axis=0)

    def planes(ref):
        for q in range(T):
            strip_ref[q * 8 : q * 8 + 8, :] = ref[0:8, q * 128 : q * 128 + 128]
            strip_ref[256 + q * 8 : 256 + q * 8 + 8, :] = ref[56:64, q * 128 : q * 128 + 128]
        y0 = strip_ref[pl.ds(0, 32, stride=8), :]
        y1 = strip_ref[pl.ds(263, 32, stride=8), :]
        f01 = pair(y0, y1)
        f23 = jnp.where(low64, ref[:, :128], ref[:, 31 * 128 :])
        f45 = mmt(jnp.concatenate(split(ref[...]), axis=0), sel_ref[...])
        return f01, f23, f45[:64] + f45[64:]

    def restrict(f01, f23, f45):
        return [jnp.sum(mm(left3(plane), w) * a, axis=0, keepdims=True)
                for plane, w, a in ((f01, w01r, a01), (f23, w23r, a23), (f45, w45r, a45))]

    rows = []
    for both in restrict(*planes(x_ref)):
        rows.extend([both[:, :128], both[:, 128:]])
    mine = jnp.concatenate(rows + [jnp.zeros((2, 128), f32)], axis=0)
    send1_ref[...] = mine
    ag_ref[me] = mine

    pl.semaphore_wait(barrier, n - 1)

    @peers
    def _(dd, dev):
        pltpu.make_async_remote_copy(src_ref=send1_ref.at[pl.ds(0, 6)], dst_ref=ag_ref.at[me, pl.ds(0, 6)],
                                     send_sem=out_s, recv_sem=ag_r,
                                     device_id=dev, device_id_type=MESH).start()

    ocopy.wait()
    m0, m1, m2 = modes_ref[0], modes_ref[1], modes_ref[2]
    am_ref[0] = left3(m0)
    am_ref[1] = left3(nt(eye64, m0))
    am_ref[2] = left3(nt(nn(qm, m1), qm))
    am_ref[3] = left3(nt(nt(qm, m1), qm))
    block = (iota((128, 128), 0) >> 6) == (iota((128, 128), 1) >> 6)
    kw_ref[0] = lanes_weights(jnp.where(block, nn(nt(dupt, m2), dup), 0.0))
    kw_ref[1] = lanes_weights(jnp.where(block, nn(dupt, nn(m2, dup)), 0.0))

    for c in range(T // CH):
        base = (c * (CH * 128))
        y = mm(am_ref[0], rows3(x_ref[:, pl.ds(base, CH * 128)]))
        stacked = jnp.concatenate([y[:, g * 128 : g * 128 + 128] for g in range(CH)], axis=0)
        s_ref[pl.ds((c * (CH * 64)), CH * 64), :] = lane_transform(stacked, kw_ref[0])

    wcopy.wait()
    for q in range(T):
        z_ref[q * 64 : q * 64 + 64, :] = w_ref[:, q * 128 : q * 128 + 128]

    def turned(ref, u):
        a = ref[pl.ds(u, 32, stride=64), :]
        b = ref[pl.ds(u + 32, 32, stride=64), :]
        return jnp.concatenate([jnp.where(low32, a, swap(b)), jnp.where(low32, swap(a), b)], axis=0)

    def middle(c, acc):
        fwd = jnp.concatenate([turned(s_ref, c * CH + g) for g in range(CH)], axis=1)
        wts = jnp.concatenate([turned(z_ref, c * CH + g) for g in range(CH)], axis=1)
        v = mm(am_ref[2], rows3(fwd))
        wv = wts * v
        prod = wv * v
        for g in range(CH):
            acc = acc + prod[:, g * 128 : g * 128 + 128]
        y = mm(am_ref[3], rows3(wv))
        for g in range(CH):
            p_ref[pl.ds((64 + (c * CH + g) * 64), 64), :] = y[:, g * 128 : g * 128 + 128]
        return acc

    gacc = jnp.zeros((64, 128), f32)
    for c in range(T // CH):
        gacc = middle(c, gacc)

    ccopy.wait()
    cap01, cap23, cap45 = planes(cap_ref)

    lcopy.wait()
    cols = cols_ref[...]
    nrow = cols.shape[0]
    nz = cols.shape[1]
    wide_cols = jnp.concatenate([jnp.broadcast_to(cols[i : i + 1, :], (nz, nz)) for i in range(nrow)], axis=0)
    kk = nrow * nz
    pick_diag = iota((kk, nz), 1) == (iota((kk, nz), 0) & (nz - 1))
    colv = jnp.sum(jnp.where(pick_diag, wide_cols.astype(f32), 0.0), axis=1, keepdims=True)
    r = iota((1, n * 8), 1)
    d = r >> 3
    f = r & 7
    own = nrow * d + f
    own = jnp.where((f == 0) & (d >= ncg), nrow * (d - ncg) + 1, own)
    own = jnp.where((f == 2) & (lax.rem(d, ncg) > 0), nrow * (d - 1) + 3, own)
    own = jnp.where(f >= 6, -1, own).astype(f32)
    g1 = jnp.where(colv == own, 1.0, 0.0)
    g1 = jnp.concatenate([g1, jnp.zeros((128 - kk, n * 8), f32)], axis=0)

    g2 = g1.T.astype(bf16)
    g2 = jnp.concatenate([g2, g2], axis=1)
    g1 = g1.astype(bf16)[: -(-kk // 16) * 16]
    bcopy.wait()

    arrived(ag_ref, 6, ag_r)
    picked = mm(g1, jnp.concatenate(split(ag_ref[...].reshape(n * 8, 128)), axis=1))
    picked = picked[:kk, :128] + picked[:kk, 128:]

    iacc = jnp.zeros((16, 1), f32)
    spread = []
    for i in range(nrow):
        pk = picked[i * nz : i * nz + nz]
        out = [jnp.zeros((16, 128), f32)] * nz
        for at in range(0, 128, 16):
            part = [blk_ref[i, k, at : at + 16, :] for k in range(nz)]
            tot = part[0] * pk[0:1]
            for k in range(1, nz):
                tot = tot + part[k] * pk[k : k + 1]
            img = jnp.sum(tot, axis=1, keepdims=True)
            iacc = iacc + img * img
            out = [o + v * img for o, v in zip(out, part)]
        spread.extend(jnp.sum(o, axis=0, keepdims=True) for o in out)
    spread = jnp.concatenate(spread + [jnp.zeros((128 - kk, 128), f32)], axis=0)
    back = mm(g2, jnp.concatenate(split(spread), axis=0))
    a2s_ref[...] = back.reshape(n, 8, 128)
    a2r_ref[me] = a2s_ref[me]

    arrived(ag_ref, 6, out_s)

    @peers
    def _(dd, dev):
        pltpu.make_async_remote_copy(src_ref=a2s_ref.at[dd, pl.ds(0, 6)], dst_ref=a2r_ref.at[me, pl.ds(0, 6)],
                                     send_sem=out_s, recv_sem=a2_r,
                                     device_id=dev, device_id_type=MESH).start()

    gpart = jnp.sum(iacc, keepdims=True) + jnp.sum(gacc, keepdims=True)

    for c in range(T // CH):
        tiles = []
        for g in range(CH):
            a = p_ref[pl.ds(64 + c * CH + g, 32, stride=64), :]
            b = p_ref[pl.ds(96 + c * CH + g, 32, stride=64), :]
            tiles.append(jnp.where(low32, a, swap(b)))
            tiles.append(jnp.where(low32, swap(a), b))
        k = lane_transform(jnp.concatenate(tiles, axis=0), kw_ref[1])
        y = jnp.concatenate([k[g * 64 : g * 64 + 64] for g in range(CH)], axis=1)
        y = mm(am_ref[1], rows3(y))
        for g in range(CH):
            l_ref[pl.ds(((c * CH + g) * 64 + 64), 64), :] = y[:, g * 128 : g * 128 + 128]

    row = iota((64, 128), 0)
    kpos = iota((64, 128), 1) & 63

    def operate(ref, q):
        at = q * 64
        x = ref[pl.ds(at + 64, 64), :]
        second = swap(x + jnp.where(low64, ref[pl.ds(at + 128, 64), :], ref[pl.ds(at, 64), :]))
        up = jnp.where(row == 0, 0.0, pltpu.roll(x, 1, 0))
        down = jnp.where(row == 63, 0.0, pltpu.roll(x, 63, 0))
        third = jnp.where(kpos == 0, 0.0, pltpu.roll(x, 1, 1)) + jnp.where(kpos == 63, 0.0, pltpu.roll(x, 127, 1))
        cols_at = pl.ds(q * 128, 128)
        img = (cap_ref[:, cols_at] + 8.2) * x - (up + down) - 0.6 * second - 2.5 * third
        img_out[:, cols_at] = img
        return x, img

    sends = (
        (s > 0, s < nsub - 1, (s - 1, t), his_ref, hi_ref, 0, 1, 0),
        (s < nsub - 1, s > 0, (s + 1, t), his_ref, hi_ref, 1, 0, 1),
        (t > 0, t < ncg - 1, (s, t - 1), hjs_ref, hj_ref, 0, 1, 2),
        (t < ncg - 1, t > 0, (s, t + 1), hjs_ref, hj_ref, 1, 0, 3),
    )

    def halo(turn, dev, src, dst, a, b, k):
        return pltpu.make_async_remote_copy(src_ref=src.at[turn, a], dst_ref=dst.at[turn, b], send_sem=dsem.at[4 * turn + k],
                                            recv_sem=h_r.at[turn, k], device_id=dev, device_id_type=MESH)

    def send_halo(turn, edge0, edge1, ref):
        his_ref[turn, 0] = edge0
        his_ref[turn, 1] = edge1
        hjs_ref[turn, 0] = jnp.where(low32, ref[64:96, :], swap(ref[96:128, :]))
        hjs_ref[turn, 1] = jnp.where(low32, swap(ref[T * 64 : T * 64 + 32, :]), ref[T * 64 + 32 : T * 64 + 64, :])
        for does, gets, dev, src, dst, a, b, k in sends:
            @pl.when(does)
            def _():
                halo(turn, dev, src, dst, a, b, k).start()

            @pl.when(jnp.logical_not(gets))
            def _():
                dst[turn, b] = jnp.zeros(dst.shape[2:], f32)

    def await_halo(turn):
        for does, gets, dev, src, dst, a, b, k in sends:
            @pl.when(gets)
            def _():
                halo(turn, dev, src, dst, a, b, k).wait_recv()

    l_ref[0:64, :] = jnp.zeros((64, 128), f32)
    l_ref[(T + 1) * 64 : (T + 2) * 64, :] = jnp.zeros((64, 128), f32)
    ledge0 = l_ref[pl.ds(64, 32, stride=64), :]
    ledge1 = l_ref[pl.ds(64 + 63, 32, stride=64), :]
    send_halo(0, ledge0, ledge1, l_ref)
    cacc = jnp.zeros((64, 128), f32)
    for q in range(T):
        value, img = operate(l_ref, q)
        cacc = cacc + value * img
    l01 = pair(ledge0, ledge1)
    l23 = jnp.where(low64, l_ref[64:128, :], l_ref[T * 64 : T * 64 + 64, :])
    image_vals = restrict(*planes(img_out))

    (n01,) = in_order([fm0t], (0, 1))
    (p45,) = in_order([nn(qm, fm1t)], (4, 5))
    ends01 = jnp.concatenate([b01[0:8], b01[56:64]], axis=0)
    x01, x23, x45 = rows3(w01.T), rows3(w23.T), rows3(w45.T)
    y01, y45 = rows3(apart(n01).T), rows3(apart(a45).T)
    inner_row = (row > 0) & (row < 63)
    inner_col = (kpos > 0) & (kpos < 63)
    last_row = row == 63
    last_col = kpos == 63
    s_low = jnp.where(s > 0, 1.0, 0.0)
    s_high = jnp.where(s < nsub - 1, 1.0, 0.0)
    t_low = jnp.where(t > 0, 0.6, 0.0)
    t_high = jnp.where(t < ncg - 1, 0.6, 0.0)

    arrived(a2r_ref, 6, a2_r)
    backs = jnp.sum(a2r_ref[...], axis=0)
    v01, v23, v45 = (jnp.concatenate([backs[f : f + 1], backs[f + 1 : f + 2]], axis=1) for f in (0, 2, 4))
    e01 = mm(left3(a01 * v01), x01)
    e23 = mm(left3(a23 * v23), x23)
    e45 = mm(left3(a45 * v45), x45)
    t01 = mm(left3(ends01 * v01), y01)
    t45 = mm(left3(p45 * v45), y45)

    def corners(e):
        lanes = iota(e.shape, 1)
        ends = jnp.where((lanes == 0) | (lanes == 127), e, 0.0)
        ends = jnp.where(lanes == 63, pltpu.roll(e, 127, 1), ends)
        return jnp.where(lanes == 64, pltpu.roll(e, 1, 1), ends)

    def whole(e, side, first, last):
        ends = jnp.where(row == 0, jnp.where(low, first, swap(last)), 0.0)
        ends = jnp.where(row == 63, jnp.where(low, swap(first), last), ends)
        return e + corners(side) + ends

    q01 = whole(e01, t45, e23[0:1], e23[63:64])
    q23 = whole(e23, e45, e01[0:1], e01[63:64])
    q45 = whole(e45, e23, t01[0:1], t01[15:16])
    k01, k23, k45 = (jnp.where(last_col, 0.0, pltpu.roll(v, 127, 1)) for v in (q01, q23, q45))
    d01 = q01 * ((cap01 + 8.2) * q01 - 5.0 * k01)
    d23 = q23 * ((cap23 + 8.2) * q23 - 5.0 * k23)
    d45 = q45 * (jnp.where(inner_col, (cap45 + 8.2) * q45, 0.0) - 1.2 * k45)
    quad = d01 + jnp.where(inner_row, d23 + d45, 0.0)
    odd = pltpu.roll(q01, 32, 0)
    after = jnp.where(row < 31, pltpu.roll(q01, 63, 0), 0.0)
    quad = quad - 1.2 * jnp.where(row < 32, odd * (q01 + after), 0.0)
    quad = quad - 2.0 * jnp.where(last_row, 0.0, q23 * pltpu.roll(q23, 63, 0))
    quad = quad - 2.0 * jnp.where(inner_col & jnp.logical_not(last_row), q45 * pltpu.roll(q45, 63, 0), 0.0)
    quad = quad - jnp.where(low, s_low, s_high) * (e01 * (2.0 * q01 - e01))
    quad = quad - jnp.where(low, t_low, t_high) * (e23 * (2.0 * q23 - e23))
    await_halo(0)
    quad = quad - (2.0 * q01 + l01) * pair(hi_ref[0, 0], hi_ref[0, 1])
    quad = quad - 0.6 * (2.0 * q23 + l23) * pair(hj_ref[0, 0], hj_ref[0, 1])
    linear = v01 * image_vals[0] + v23 * image_vals[1] + v45 * image_vals[2]
    total = jnp.sum(cacc + quad, keepdims=True) + 2.0 * jnp.sum(linear, keepdims=True)
    lanes = iota((1, 128), 1)
    corner = (lanes == 0) | (lanes == 127)
    corner = corner | (lanes == 63) | (lanes == 64)
    for at, (across, along) in enumerate(((e23[0:1], e45[0:1]), (e23[63:64], e45[63:64]),
                                          (e01[0:1], t45[0:1]), (e01[63:64], t45[63:64]))):
        cs_ref[2 * at : 2 * at + 1, :] = across + corners(along)
        rest = jnp.where(corner, 0.0, along)
        if at == 0:
            rest = jnp.where(lanes == 0, total, jnp.where(lanes == 127, gpart, rest))
        cs_ref[2 * at + 1 : 2 * at + 2, :] = rest
    cr_ref[me] = cs_ref[...]

    arrived(a2r_ref, 6, out_s)

    def send_sum(dd, dev):
        pltpu.make_async_remote_copy(src_ref=cs_ref, dst_ref=cr_ref.at[me], send_sem=out_s, recv_sem=c_r,
                                     device_id=dev, device_id_type=MESH).start()

    for d in range(ncg):
        @pl.when(me != d)
        def _():
            send_sum(d, (0, d))

    @peers
    def _(dd, dev):
        @pl.when(dd >= ncg)
        def _():
            send_sum(dd, dev)

    eh, el = split(e45)
    eh = jnp.concatenate([eh, el], axis=0)

    for c in range(T // CH):
        base = (c * (CH * 128))
        add = mm(eh, sel_ref[:, pl.ds(base, CH * 128)])
        for g in range(CH):
            at = ((c * CH + g) * 64)
            tile = add[:64, g * 128 : g * 128 + 128] + add[64:, g * 128 : g * 128 + 128]
            p_ref[pl.ds(at + 64, 64), :] = l_ref[pl.ds(at + 64, 64), :] + tile

    p_ref[64:128, :] += jnp.where(low64, e23, 0.0)
    p_ref[T * 64 : T * 64 + 64, :] += jnp.where(low64, 0.0, e23)
    top, bottom = e01[:32], e01[32:]
    edge0 = p_ref[pl.ds(64, 32, stride=64), :] + jnp.where(low32, top, swap(bottom))
    edge1 = p_ref[pl.ds(64 + 63, 32, stride=64), :] + jnp.where(low32, swap(top), bottom)
    p_ref[pl.ds(64, 32, stride=64), :] = edge0
    p_ref[pl.ds(64 + 63, 32, stride=64), :] = edge1

    p_ref[0:64, :] = jnp.zeros((64, 128), f32)
    p_ref[(T + 1) * 64 : (T + 2) * 64, :] = jnp.zeros((64, 128), f32)

    for q in range(T):
        value, _ = operate(p_ref, q)
        p_out[:, q * 128 : q * 128 + 128] = value
    send_halo(1, edge0, edge1, p_ref)
    await_halo(1)
    outside = 0.6 * pair(hj_ref[1, 0], hj_ref[1, 1])
    img_out[:, :128] = img_out[:, :128] - jnp.where(low64, outside, 0.0)
    img_out[:, (T - 1) * 128 :] = img_out[:, (T - 1) * 128 :] - jnp.where(low64, 0.0, outside)
    for q in range(T):
        at = slice(q * 128, q * 128 + 128)
        img_out[0:1, at] = img_out[0:1, at] - hi_ref[1, 0, q : q + 1, :]
        img_out[63:64, at] = img_out[63:64, at] - hi_ref[1, 1, q : q + 1, :]

    arrived(cr_ref, 8, c_r)
    both = cr_ref[0]
    first = jnp.zeros((8, 128), f32)
    second = jnp.zeros((8, 128), f32)
    for d in range(n):
        high = pltpu.roll(cr_ref[d], 6, 0)
        if d > 0:
            both = both + cr_ref[d]
        if d + ncg < n:
            first = first + high * cr_ref[d + ncg]
        if (d + 1) % ncg:
            second = second + high * cr_ref[d + 1]
    row8 = iota((8, 128), 0)
    lane8 = iota((8, 128), 1)
    cross = jnp.where(row8 < 2, first, jnp.where((row8 == 4) | (row8 == 5), 0.6 * second, 0.0))
    inside = ((lane8 & 63) > 0) & ((lane8 & 63) < 63)
    cross = jnp.where(inside | ((row8 & 1) == 0), -2.0 * cross, 0.0)
    curv = jnp.sum(cross, keepdims=True) + both[1:2, 0:1]
    gamma = both[1:2, 127:128]
    alpha_out[...] = gamma / curv

    arrived(cr_ref, 8, out_s)
    for turn in range(2):
        for does, gets, dev, src, dst, a, b, k in sends:
            @pl.when(does)
            def _():
                halo(turn, dev, src, dst, a, b, k).wait_send()


def finish(p_ref, img_ref, x_ref, alpha_ref, sol_any, res_any, sol_ref, res_ref, sem):
    a = alpha_ref[...]
    for c in range(4):
        at = pl.ds(c * 16, 16)
        sol_ref[at, :] = a * p_ref[at, :]
        pltpu.make_async_copy(sol_ref.at[at], sol_any.at[at], sem.at[0]).start()
        res_ref[at, :] = x_ref[at, :] - a * img_ref[at, :]
        pltpu.make_async_copy(res_ref.at[at], res_any.at[at], sem.at[1]).start()
    pltpu.make_async_copy(sol_ref, sol_any, sem.at[0]).wait()
    pltpu.make_async_copy(res_ref, res_any, sem.at[1]).wait()


def body(nsub, ncg, source, capacity, fd_weights, fd_modes, face_modes, coarse_map, fsai_cols, fsai_blocks):
    n = nsub * ncg
    nrow, nz = fsai_cols.shape
    vm = pl.BlockSpec(memory_space=pltpu.VMEM)
    hbm = pl.BlockSpec(memory_space=pltpu.HBM)
    field = jax.ShapeDtypeStruct(source.shape, f32)
    V = pltpu.VMEM
    dma = pltpu.SemaphoreType.DMA
    p, img, x, alpha = pl.pallas_call(
        functools.partial(kernel, nsub, ncg),
        out_shape=(field, field, field, jax.ShapeDtypeStruct((1, 1), f32)),
        in_specs=[hbm] * 8,
        out_specs=(vm, vm, vm, vm),
        scratch_shapes=[
            V(fd_modes.shape, f32),
            V((2, 64, 128), f32),
            V((6, 1, 128), jnp.int32),
            V(fsai_cols.shape, jnp.int32),
            V((T * 64, 128), f32),
            V((T * 64, 128), f32),
            V((64, T * 128), f32),
            V(((T + 2) * 64, 128), f32),
            V((64, T * 128), f32),
            V(fsai_blocks.shape, f32),
            V((128, T * 128), bf16),
            V((4, 64, 192), bf16),
            V((2, 256, 256), bf16),
            V((n, 8, 128), f32),
            V((8, 128), f32),
            V((n, 8, 128), f32),
            V((n, 8, 128), f32),
            V((2, 2, 32, 128), f32),
            V((2, 2, 32, 128), f32),
            V((2, 2, 32, 128), f32),
            V((2, 2, 32, 128), f32),
            V((8, 128), f32),
            V((n, 8, 128), f32),
            V(((T + 2) * 64, 128), f32),
            V((512, 128), f32),
            dma((8,)),
            dma, dma, dma, dma((2, 4)), dma,
        ],
        compiler_params=pltpu.CompilerParams(collective_id=0, has_side_effects=True,
                                             vmem_limit_bytes=48 * 1024 * 1024),
        cost_estimate=pl.CostEstimate(flops=10**9, bytes_accessed=8 * 2**20, transcendentals=0),
        name="step",
    )(*(pltpu.with_memory_space_constraint(v, pltpu.HBM) for v in (
        source, fd_modes, jnp.swapaxes(face_modes, 1, 2), coarse_map.reshape(-1, 1, coarse_map.shape[-1]),
        fsai_cols, capacity, fd_weights, fsai_blocks)))
    return pl.pallas_call(
        finish,
        out_shape=(field, field),
        in_specs=[vm] * 4,
        out_specs=(hbm, hbm),
        scratch_shapes=[V(source.shape, f32), V(source.shape, f32), dma((2,))],
        cost_estimate=pl.CostEstimate(flops=2**20, bytes_accessed=2 * 2**20, transcendentals=0),
        name="finish",
    )(*(pltpu.with_memory_space_constraint(v, pltpu.VMEM) for v in (p, img, x, alpha)))


def solution(mesh):
    in_specs = (
        P("sub", "cgrp"),
        P("sub", "cgrp"),
        P("sub", "cgrp"),
        P(),
        P(),
        P("sub", "cgrp", None, None),
        P(("sub", "cgrp"), None),
        P(("sub", "cgrp"), None, None, None),
    )
    out_specs = (P("sub", "cgrp"), P("sub", "cgrp"))
    step = functools.partial(body, mesh.shape["sub"], mesh.shape["cgrp"])
    return jax.shard_map(step, mesh=mesh, in_specs=in_specs, out_specs=out_specs, check_vma=False)
```

```python
import functools
import jax
import jax.numpy as jnp
from jax import lax
from jax.experimental import pallas as pl
from jax.experimental.pallas import tpu as pltpu
from jax.sharding import PartitionSpec as P

C = 64
T = 32
CH = 8
f32 = jnp.float32
bf16 = jnp.bfloat16
HI = lax.Precision.HIGHEST
MESH = pl.DeviceIdType.MESH


def nn(a, b):
    return lax.dot_general(a, b, (((1,), (0,)), ((), ())), precision=HI, preferred_element_type=f32)


def nt(a, b):
    return lax.dot_general(a, b, (((1,), (1,)), ((), ())), precision=HI, preferred_element_type=f32)


def mm(a, b):
    return lax.dot_general(a, b, (((1,), (0,)), ((), ())), preferred_element_type=f32)


def mmt(a, b):
    return lax.dot_general(a, b, (((1,), (1,)), ((), ())), preferred_element_type=f32)


def split(x):
    hi = x.astype(bf16)
    return hi, (x - hi.astype(f32)).astype(bf16)


def iota(shape, dim):
    return lax.broadcasted_iota(jnp.int32, shape, dim)


def left3(m):
    hi, lo = split(m)
    return jnp.concatenate([hi, lo, hi], axis=1)


def rows3(x):
    hi, lo = split(x)
    return jnp.concatenate([hi, hi, lo], axis=0)


def lanes_weights(k):
    hi, lo = split(k)
    top = jnp.concatenate([hi, lo], axis=1)
    bottom = jnp.concatenate([hi, jnp.zeros_like(lo)], axis=1)
    return jnp.concatenate([top, bottom], axis=0)


def lane_transform(x, w):
    hi, lo = split(x)
    r = mm(jnp.concatenate([hi, lo], axis=1), w)
    return r[:, :128] + r[:, 128:]


def kernel(nsub, ncg, x_any, modes_any, face_any, map_any, cols_any, cap_any, wt_any, blk_any,
           p_out, img_out, x_ref, alpha_out,
           modes_ref, face_ref, map_ref, cols_ref,
           s_ref, z_ref, w_ref, p_ref, cap_ref, blk_ref, sel_ref, am_ref, kw_ref,
           ag_ref, send1_ref, a2s_ref, a2r_ref,
           hi_ref, his_ref, hj_ref, hjs_ref, cs_ref, cr_ref, l_ref, strip_ref,
           dsem, out_s, ag_r, a2_r, h_r, c_r):
    n = nsub * ncg
    s = lax.axis_index("sub")
    t = lax.axis_index("cgrp")
    me = s * ncg + t

    def peer(o):
        d = lax.rem(me + o, n)
        return d, (lax.div(d, ncg), lax.rem(d, ncg))

    early = [pltpu.make_async_copy(src, dst, dsem.at[k]) for k, (src, dst) in enumerate((
        (face_any, face_ref), (map_any, map_ref), (x_any, x_ref), (modes_any, modes_ref), (cols_any, cols_ref),
        (wt_any, w_ref), (blk_any, blk_ref), (cap_any, cap_ref)))]
    for copy in early[:5]:
        copy.start()
    fcopy, mcopy, xcopy, ocopy, lcopy, wcopy, bcopy, ccopy = early

    def mirrors(v, size):
        out = [v]
        while len(out) < size:
            bit = len(out)
            flip = bit - 2 * bit * lax.rem(lax.div(v, bit), 2)
            out = out + [o + flip for o in out]
        return out

    if n <= 32:
        to_s, to_t = mirrors(s, nsub), mirrors(t, ncg)
        order = [(a, b) for a in range(nsub) for b in range(ncg) if a or b]
        order.sort(key=lambda ab: -(min(ab[0], 2) + (ab[1] >> 1 & 1) + (ab[1] >> 2 & 1)))

    def peers(step):
        if n > 32:
            @pl.loop(1, n)
            def _(o):
                step(*peer(o))
        else:
            for a, b in order:
                step(to_s[a] * ncg + to_t[b], (to_s[a], to_t[b]))

    def arrived(ref, rows, sem):
        part = ref.at[pl.ds(0, n - 1), pl.ds(0, rows)]
        pltpu.make_async_copy(part, part, sem).wait()

    ag_ref[...] = jnp.zeros_like(ag_ref)
    a2r_ref[...] = jnp.zeros_like(a2r_ref)
    barrier = pltpu.get_barrier_semaphore()

    @pl.loop(1, n)
    def _(o):
        _, dev = peer(o)
        pl.semaphore_signal(barrier, inc=1, device_id=dev, device_id_type=MESH)

    lane = iota((1, 128), 1)
    low = lane < 64
    low32 = jnp.broadcast_to(low, (32, 128))
    low64 = jnp.broadcast_to(low, (64, 128))

    def swap(a):
        return pltpu.roll(a, 64, 1)

    @pl.loop(0, 8)
    def _(c):
        r = iota((128, 512), 0)
        col = iota((128, 512), 1) + c * 512
        hit = ((col >> 6) == (r & 63)) & ((col & 63) == 63 * (r >> 6))
        sel_ref[:, pl.ds(pl.multiple_of(c * 512, 512), 512)] = jnp.where(hit, 1.0, 0.0).astype(bf16)

    fcopy.wait()
    mcopy.wait()
    fm0t = face_ref[0]
    fm1t = face_ref[1]
    r64 = iota((64, 64), 0)
    c64 = iota((64, 64), 1)
    eye64 = jnp.where(r64 == c64, 1.0, 0.0)
    qm = jnp.where(c64 == 2 * (r64 & 31) + (r64 >> 5), 1.0, 0.0)
    dup = jnp.where((iota((64, 128), 1) & 63) == iota((64, 128), 0), 1.0, 0.0)
    dupt = jnp.where((iota((128, 64), 0) & 63) == iota((128, 64), 1), 1.0, 0.0)
    eye128 = jnp.where(iota((128, 128), 0) == iota((128, 128), 1), 1.0, 0.0)
    fm0pt = nn(qm, fm0t)

    mapf = [(map_ref[f] & 127).astype(f32) for f in range(6)]
    mapf = jnp.concatenate(mapf + [jnp.zeros((2, 128), f32)], axis=0)
    mapt = mmt(eye128.astype(bf16), mapf.astype(bf16))
    lanef = iota((128, 128), 1).astype(f32)
    hot = [jnp.where(mapt[:, f : f + 1] == lanef, 1.0, 0.0).astype(bf16) for f in range(6)]

    def in_order(mats, faces):
        m = jnp.concatenate(mats, axis=0)
        hi, lo = split(m)
        rest = (m - hi.astype(f32) - lo.astype(f32)).astype(bf16)
        size = m.shape[0]
        r = mm(jnp.concatenate([hi, lo, rest], axis=0), jnp.concatenate([hot[f] for f in faces], axis=1))
        r = r[:size] + r[size : 2 * size] + r[2 * size :]
        return [r[k * 64 : k * 64 + 64] for k in range(len(mats))]

    def apart(m):
        zero = jnp.zeros((64, 128), f32)
        return jnp.concatenate([jnp.concatenate([m[:, :128], zero], axis=1),
                                jnp.concatenate([zero, m[:, 128:]], axis=1)], axis=0)

    a01, b01 = in_order([fm0pt, fm1t], (0, 1))
    a25, b25 = in_order([fm0t, fm1t], (2, 3, 4, 5))
    a23, a45, b23, b45 = a25[:, :256], a25[:, 256:], b25[:, :256], b25[:, 256:]
    w01, w23, w45 = apart(b01), apart(b23), apart(b45)
    w01r, w23r, w45r = rows3(w01), rows3(w23), rows3(w45)

    xcopy.wait()
    for copy in early[5:]:
        copy.start()

    def pair(a, b):
        return jnp.concatenate([jnp.where(low32, a, swap(b)), jnp.where(low32, swap(a), b)], axis=0)

    def planes(ref):
        for q in range(T):
            strip_ref[q * 8 : q * 8 + 8, :] = ref[0:8, q * 128 : q * 128 + 128]
            strip_ref[256 + q * 8 : 256 + q * 8 + 8, :] = ref[56:64, q * 128 : q * 128 + 128]
        y0 = strip_ref[pl.ds(0, 32, stride=8), :]
        y1 = strip_ref[pl.ds(263, 32, stride=8), :]
        f01 = pair(y0, y1)
        f23 = jnp.where(low64, ref[:, :128], ref[:, 31 * 128 :])
        f45 = mmt(jnp.concatenate(split(ref[...]), axis=0), sel_ref[...])
        return f01, f23, f45[:64] + f45[64:]

    def restrict(f01, f23, f45):
        return [jnp.sum(mm(left3(plane), w) * a, axis=0, keepdims=True)
                for plane, w, a in ((f01, w01r, a01), (f23, w23r, a23), (f45, w45r, a45))]

    rows = []
    for both in restrict(*planes(x_ref)):
        rows.extend([both[:, :128], both[:, 128:]])
    mine = jnp.concatenate(rows + [jnp.zeros((2, 128), f32)], axis=0)
    send1_ref[...] = mine
    ag_ref[me] = mine

    pl.semaphore_wait(barrier, n - 1)

    @peers
    def _(dd, dev):
        pltpu.make_async_remote_copy(src_ref=send1_ref.at[pl.ds(0, 6)], dst_ref=ag_ref.at[me, pl.ds(0, 6)],
                                     send_sem=out_s, recv_sem=ag_r,
                                     device_id=dev, device_id_type=MESH).start()

    ocopy.wait()
    m0, m1, m2 = modes_ref[0], modes_ref[1], modes_ref[2]
    am_ref[0] = left3(m0)
    am_ref[1] = left3(nt(eye64, m0))
    am_ref[2] = left3(nt(nn(qm, m1), qm))
    am_ref[3] = left3(nt(nt(qm, m1), qm))
    block = (iota((128, 128), 0) >> 6) == (iota((128, 128), 1) >> 6)
    kw_ref[0] = lanes_weights(jnp.where(block, nn(nt(dupt, m2), dup), 0.0))
    kw_ref[1] = lanes_weights(jnp.where(block, nn(dupt, nn(m2, dup)), 0.0))

    for c in range(T // CH):
        base = (c * (CH * 128))
        y = mm(am_ref[0], rows3(x_ref[:, pl.ds(base, CH * 128)]))
        stacked = jnp.concatenate([y[:, g * 128 : g * 128 + 128] for g in range(CH)], axis=0)
        s_ref[pl.ds((c * (CH * 64)), CH * 64), :] = lane_transform(stacked, kw_ref[0])

    wcopy.wait()
    for q in range(T):
        z_ref[q * 64 : q * 64 + 64, :] = w_ref[:, q * 128 : q * 128 + 128]

    def turned(ref, u):
        a = ref[pl.ds(u, 32, stride=64), :]
        b = ref[pl.ds(u + 32, 32, stride=64), :]
        return jnp.concatenate([jnp.where(low32, a, swap(b)), jnp.where(low32, swap(a), b)], axis=0)

    def middle(c, acc):
        fwd = jnp.concatenate([turned(s_ref, c * CH + g) for g in range(CH)], axis=1)
        wts = jnp.concatenate([turned(z_ref, c * CH + g) for g in range(CH)], axis=1)
        v = mm(am_ref[2], rows3(fwd))
        wv = wts * v
        prod = wv * v
        for g in range(CH):
            acc = acc + prod[:, g * 128 : g * 128 + 128]
        y = mm(am_ref[3], rows3(wv))
        for g in range(CH):
            p_ref[pl.ds((64 + (c * CH + g) * 64), 64), :] = y[:, g * 128 : g * 128 + 128]
        return acc

    gacc = jnp.zeros((64, 128), f32)
    for c in range(T // CH):
        gacc = middle(c, gacc)

    ccopy.wait()
    cap01, cap23, cap45 = planes(cap_ref)

    lcopy.wait()
    cols = cols_ref[...]
    nrow = cols.shape[0]
    nz = cols.shape[1]
    wide_cols = jnp.concatenate([jnp.broadcast_to(cols[i : i + 1, :], (nz, nz)) for i in range(nrow)], axis=0)
    kk = nrow * nz
    pick_diag = iota((kk, nz), 1) == (iota((kk, nz), 0) & (nz - 1))
    colv = jnp.sum(jnp.where(pick_diag, wide_cols.astype(f32), 0.0), axis=1, keepdims=True)
    r = iota((1, n * 8), 1)
    d = r >> 3
    f = r & 7
    own = nrow * d + f
    own = jnp.where((f == 0) & (d >= ncg), nrow * (d - ncg) + 1, own)
    own = jnp.where((f == 2) & (lax.rem(d, ncg) > 0), nrow * (d - 1) + 3, own)
    own = jnp.where(f >= 6, -1, own).astype(f32)
    g1 = jnp.where(colv == own, 1.0, 0.0)
    g1 = jnp.concatenate([g1, jnp.zeros((128 - kk, n * 8), f32)], axis=0)

    g2 = g1.T.astype(bf16)
    g2 = jnp.concatenate([g2, g2], axis=1)
    g1 = g1.astype(bf16)[: -(-kk // 16) * 16]
    bcopy.wait()

    arrived(ag_ref, 6, ag_r)
    picked = mm(g1, jnp.concatenate(split(ag_ref[...].reshape(n * 8, 128)), axis=1))
    picked = picked[:kk, :128] + picked[:kk, 128:]

    iacc = jnp.zeros((16, 1), f32)
    spread = []
    for i in range(nrow):
        pk = picked[i * nz : i * nz + nz]
        out = [jnp.zeros((16, 128), f32)] * nz
        for at in range(0, 128, 16):
            part = [blk_ref[i, k, at : at + 16, :] for k in range(nz)]
            tot = part[0] * pk[0:1]
            for k in range(1, nz):
                tot = tot + part[k] * pk[k : k + 1]
            img = jnp.sum(tot, axis=1, keepdims=True)
            iacc = iacc + img * img
            out = [o + v * img for o, v in zip(out, part)]
        spread.extend(jnp.sum(o, axis=0, keepdims=True) for o in out)
    spread = jnp.concatenate(spread + [jnp.zeros((128 - kk, 128), f32)], axis=0)
    back = mm(g2, jnp.concatenate(split(spread), axis=0))
    a2s_ref[...] = back.reshape(n, 8, 128)
    a2r_ref[me] = a2s_ref[me]

    arrived(ag_ref, 6, out_s)

    @peers
    def _(dd, dev):
        pltpu.make_async_remote_copy(src_ref=a2s_ref.at[dd, pl.ds(0, 6)], dst_ref=a2r_ref.at[me, pl.ds(0, 6)],
                                     send_sem=out_s, recv_sem=a2_r,
                                     device_id=dev, device_id_type=MESH).start()

    gpart = jnp.sum(iacc, keepdims=True) + jnp.sum(gacc, keepdims=True)

    for c in range(T // CH):
        tiles = []
        for g in range(CH):
            a = p_ref[pl.ds(64 + c * CH + g, 32, stride=64), :]
            b = p_ref[pl.ds(96 + c * CH + g, 32, stride=64), :]
            tiles.append(jnp.where(low32, a, swap(b)))
            tiles.append(jnp.where(low32, swap(a), b))
        k = lane_transform(jnp.concatenate(tiles, axis=0), kw_ref[1])
        y = jnp.concatenate([k[g * 64 : g * 64 + 64] for g in range(CH)], axis=1)
        y = mm(am_ref[1], rows3(y))
        for g in range(CH):
            l_ref[pl.ds(((c * CH + g) * 64 + 64), 64), :] = y[:, g * 128 : g * 128 + 128]

    row = iota((64, 128), 0)
    kpos = iota((64, 128), 1) & 63

    def operate(ref, q):
        at = q * 64
        x = ref[pl.ds(at + 64, 64), :]
        second = swap(x + jnp.where(low64, ref[pl.ds(at + 128, 64), :], ref[pl.ds(at, 64), :]))
        up = jnp.where(row == 0, 0.0, pltpu.roll(x, 1, 0))
        down = jnp.where(row == 63, 0.0, pltpu.roll(x, 63, 0))
        third = jnp.where(kpos == 0, 0.0, pltpu.roll(x, 1, 1)) + jnp.where(kpos == 63, 0.0, pltpu.roll(x, 127, 1))
        cols_at = pl.ds(q * 128, 128)
        img = (cap_ref[:, cols_at] + 8.2) * x - (up + down) - 0.6 * second - 2.5 * third
        img_out[:, cols_at] = img
        return x, img

    sends = (
        (s > 0, s < nsub - 1, (s - 1, t), his_ref, hi_ref, 0, 1, 0),
        (s < nsub - 1, s > 0, (s + 1, t), his_ref, hi_ref, 1, 0, 1),
        (t > 0, t < ncg - 1, (s, t - 1), hjs_ref, hj_ref, 0, 1, 2),
        (t < ncg - 1, t > 0, (s, t + 1), hjs_ref, hj_ref, 1, 0, 3),
    )

    def halo(turn, dev, src, dst, a, b, k):
        return pltpu.make_async_remote_copy(src_ref=src.at[turn, a], dst_ref=dst.at[turn, b], send_sem=dsem.at[4 * turn + k],
                                            recv_sem=h_r.at[turn, k], device_id=dev, device_id_type=MESH)

    def send_halo(turn, edge0, edge1, ref):
        his_ref[turn, 0] = edge0
        his_ref[turn, 1] = edge1
        hjs_ref[turn, 0] = jnp.where(low32, ref[64:96, :], swap(ref[96:128, :]))
        hjs_ref[turn, 1] = jnp.where(low32, swap(ref[T * 64 : T * 64 + 32, :]), ref[T * 64 + 32 : T * 64 + 64, :])
        for does, gets, dev, src, dst, a, b, k in sends:
            @pl.when(does)
            def _():
                halo(turn, dev, src, dst, a, b, k).start()

            @pl.when(jnp.logical_not(gets))
            def _():
                dst[turn, b] = jnp.zeros(dst.shape[2:], f32)

    def await_halo(turn):
        for does, gets, dev, src, dst, a, b, k in sends:
            @pl.when(gets)
            def _():
                halo(turn, dev, src, dst, a, b, k).wait_recv()

    l_ref[0:64, :] = jnp.zeros((64, 128), f32)
    l_ref[(T + 1) * 64 : (T + 2) * 64, :] = jnp.zeros((64, 128), f32)
    ledge0 = l_ref[pl.ds(64, 32, stride=64), :]
    ledge1 = l_ref[pl.ds(64 + 63, 32, stride=64), :]
    send_halo(0, ledge0, ledge1, l_ref)
    cacc = jnp.zeros((64, 128), f32)
    for q in range(T):
        value, img = operate(l_ref, q)
        cacc = cacc + value * img
    l01 = pair(ledge0, ledge1)
    l23 = jnp.where(low64, l_ref[64:128, :], l_ref[T * 64 : T * 64 + 64, :])
    image_vals = restrict(*planes(img_out))

    (n01,) = in_order([fm0t], (0, 1))
    (p45,) = in_order([nn(qm, fm1t)], (4, 5))
    ends01 = jnp.concatenate([b01[0:8], b01[56:64]], axis=0)
    x01, x23, x45 = rows3(w01.T), rows3(w23.T), rows3(w45.T)
    y01, y45 = rows3(apart(n01).T), rows3(apart(a45).T)
    inner_row = (row > 0) & (row < 63)
    inner_col = (kpos > 0) & (kpos < 63)
    last_row = row == 63
    last_col = kpos == 63
    s_low = jnp.where(s > 0, 1.0, 0.0)
    s_high = jnp.where(s < nsub - 1, 1.0, 0.0)
    t_low = jnp.where(t > 0, 0.6, 0.0)
    t_high = jnp.where(t < ncg - 1, 0.6, 0.0)

    arrived(a2r_ref, 6, a2_r)
    def total_of(parts):
        while len(parts) > 1:
            parts = [sum(parts[k : k + 2][1:], parts[k]) for k in range(0, len(parts), 2)]
        return parts[0]

    backs = total_of([a2r_ref[d] for d in range(n)])
    v01, v23, v45 = (jnp.concatenate([backs[f : f + 1], backs[f + 1 : f + 2]], axis=1) for f in (0, 2, 4))
    e01 = mm(left3(a01 * v01), x01)
    e23 = mm(left3(a23 * v23), x23)
    e45 = mm(left3(a45 * v45), x45)
    t01 = mm(left3(ends01 * v01), y01)
    t45 = mm(left3(p45 * v45), y45)

    def corners(e):
        lanes = iota(e.shape, 1)
        ends = jnp.where((lanes == 0) | (lanes == 127), e, 0.0)
        ends = jnp.where(lanes == 63, pltpu.roll(e, 127, 1), ends)
        return jnp.where(lanes == 64, pltpu.roll(e, 1, 1), ends)

    def whole(e, side, first, last):
        ends = jnp.where(row == 0, jnp.where(low, first, swap(last)), 0.0)
        ends = jnp.where(row == 63, jnp.where(low, swap(first), last), ends)
        return e + corners(side) + ends

    q01 = whole(e01, t45, e23[0:1], e23[63:64])
    q23 = whole(e23, e45, e01[0:1], e01[63:64])
    q45 = whole(e45, e23, t01[0:1], t01[15:16])
    k01, k23, k45 = (jnp.where(last_col, 0.0, pltpu.roll(v, 127, 1)) for v in (q01, q23, q45))
    d01 = q01 * ((cap01 + 8.2) * q01 - 5.0 * k01)
    d23 = q23 * ((cap23 + 8.2) * q23 - 5.0 * k23)
    d45 = q45 * (jnp.where(inner_col, (cap45 + 8.2) * q45, 0.0) - 1.2 * k45)
    quad = d01 + jnp.where(inner_row, d23 + d45, 0.0)
    odd = pltpu.roll(q01, 32, 0)
    after = jnp.where(row < 31, pltpu.roll(q01, 63, 0), 0.0)
    quad = quad - 1.2 * jnp.where(row < 32, odd * (q01 + after), 0.0)
    quad = quad - 2.0 * jnp.where(last_row, 0.0, q23 * pltpu.roll(q23, 63, 0))
    quad = quad - 2.0 * jnp.where(inner_col & jnp.logical_not(last_row), q45 * pltpu.roll(q45, 63, 0), 0.0)
    quad = quad - jnp.where(low, s_low, s_high) * (e01 * (2.0 * q01 - e01))
    quad = quad - jnp.where(low, t_low, t_high) * (e23 * (2.0 * q23 - e23))
    await_halo(0)
    quad = quad - (2.0 * q01 + l01) * pair(hi_ref[0, 0], hi_ref[0, 1])
    quad = quad - 0.6 * (2.0 * q23 + l23) * pair(hj_ref[0, 0], hj_ref[0, 1])
    linear = v01 * image_vals[0] + v23 * image_vals[1] + v45 * image_vals[2]
    total = jnp.sum(cacc + quad, keepdims=True) + 2.0 * jnp.sum(linear, keepdims=True)
    lanes = iota((1, 128), 1)
    corner = (lanes == 0) | (lanes == 127)
    corner = corner | (lanes == 63) | (lanes == 64)
    for at, (across, along) in enumerate(((e23[0:1], e45[0:1]), (e23[63:64], e45[63:64]),
                                          (e01[0:1], t45[0:1]), (e01[63:64], t45[63:64]))):
        cs_ref[2 * at : 2 * at + 1, :] = across + corners(along)
        rest = jnp.where(corner, 0.0, along)
        if at == 0:
            rest = jnp.where(lanes == 0, total, jnp.where(lanes == 127, gpart, rest))
        cs_ref[2 * at + 1 : 2 * at + 2, :] = rest
    cr_ref[me] = cs_ref[...]

    arrived(a2r_ref, 6, out_s)

    def send_sum(dd, dev):
        pltpu.make_async_remote_copy(src_ref=cs_ref, dst_ref=cr_ref.at[me], send_sem=out_s, recv_sem=c_r,
                                     device_id=dev, device_id_type=MESH).start()

    for d in range(ncg):
        @pl.when(me != d)
        def _():
            send_sum(d, (0, d))

    @peers
    def _(dd, dev):
        @pl.when(dd >= ncg)
        def _():
            send_sum(dd, dev)

    eh, el = split(e45)
    eh = jnp.concatenate([eh, el], axis=0)

    for c in range(T // CH):
        base = (c * (CH * 128))
        add = mm(eh, sel_ref[:, pl.ds(base, CH * 128)])
        for g in range(CH):
            at = ((c * CH + g) * 64)
            tile = add[:64, g * 128 : g * 128 + 128] + add[64:, g * 128 : g * 128 + 128]
            p_ref[pl.ds(at + 64, 64), :] = l_ref[pl.ds(at + 64, 64), :] + tile

    p_ref[64:128, :] += jnp.where(low64, e23, 0.0)
    p_ref[T * 64 : T * 64 + 64, :] += jnp.where(low64, 0.0, e23)
    top, bottom = e01[:32], e01[32:]
    edge0 = p_ref[pl.ds(64, 32, stride=64), :] + jnp.where(low32, top, swap(bottom))
    edge1 = p_ref[pl.ds(64 + 63, 32, stride=64), :] + jnp.where(low32, swap(top), bottom)
    p_ref[pl.ds(64, 32, stride=64), :] = edge0
    p_ref[pl.ds(64 + 63, 32, stride=64), :] = edge1

    p_ref[0:64, :] = jnp.zeros((64, 128), f32)
    p_ref[(T + 1) * 64 : (T + 2) * 64, :] = jnp.zeros((64, 128), f32)

    for q in range(T):
        value, _ = operate(p_ref, q)
        p_out[:, q * 128 : q * 128 + 128] = value
    send_halo(1, edge0, edge1, p_ref)
    await_halo(1)
    outside = 0.6 * pair(hj_ref[1, 0], hj_ref[1, 1])
    img_out[:, :128] = img_out[:, :128] - jnp.where(low64, outside, 0.0)
    img_out[:, (T - 1) * 128 :] = img_out[:, (T - 1) * 128 :] - jnp.where(low64, 0.0, outside)
    for q in range(T):
        at = slice(q * 128, q * 128 + 128)
        img_out[0:1, at] = img_out[0:1, at] - hi_ref[1, 0, q : q + 1, :]
        img_out[63:64, at] = img_out[63:64, at] - hi_ref[1, 1, q : q + 1, :]

    arrived(cr_ref, 8, c_r)
    got = [cr_ref[d] for d in range(n)]
    high = [pltpu.roll(v, 6, 0) for v in got]
    both = total_of(got)
    first = total_of([high[d] * got[d + ncg] for d in range(n - ncg)])
    second = total_of([high[d] * got[d + 1] for d in range(n) if (d + 1) % ncg])
    row8 = iota((8, 128), 0)
    lane8 = iota((8, 128), 1)
    cross = jnp.where(row8 < 2, first, jnp.where((row8 == 4) | (row8 == 5), 0.6 * second, 0.0))
    inside = ((lane8 & 63) > 0) & ((lane8 & 63) < 63)
    cross = jnp.where(inside | ((row8 & 1) == 0), -2.0 * cross, 0.0)
    curv = jnp.sum(cross, keepdims=True) + both[1:2, 0:1]
    gamma = both[1:2, 127:128]
    alpha_out[...] = gamma / curv

    arrived(cr_ref, 8, out_s)
    for turn in range(2):
        for does, gets, dev, src, dst, a, b, k in sends:
            @pl.when(does)
            def _():
                halo(turn, dev, src, dst, a, b, k).wait_send()


def finish(p_ref, img_ref, x_ref, alpha_ref, sol_any, res_any, sol_ref, res_ref, sem):
    a = alpha_ref[...]
    for c in range(4):
        at = pl.ds(c * 16, 16)
        sol_ref[at, :] = a * p_ref[at, :]
        pltpu.make_async_copy(sol_ref.at[at], sol_any.at[at], sem.at[0]).start()
        res_ref[at, :] = x_ref[at, :] - a * img_ref[at, :]
        pltpu.make_async_copy(res_ref.at[at], res_any.at[at], sem.at[1]).start()
    pltpu.make_async_copy(sol_ref, sol_any, sem.at[0]).wait()
    pltpu.make_async_copy(res_ref, res_any, sem.at[1]).wait()


def body(nsub, ncg, source, capacity, fd_weights, fd_modes, face_modes, coarse_map, fsai_cols, fsai_blocks):
    n = nsub * ncg
    nrow, nz = fsai_cols.shape
    vm = pl.BlockSpec(memory_space=pltpu.VMEM)
    hbm = pl.BlockSpec(memory_space=pltpu.HBM)
    field = jax.ShapeDtypeStruct(source.shape, f32)
    V = pltpu.VMEM
    dma = pltpu.SemaphoreType.DMA
    p, img, x, alpha = pl.pallas_call(
        functools.partial(kernel, nsub, ncg),
        out_shape=(field, field, field, jax.ShapeDtypeStruct((1, 1), f32)),
        in_specs=[hbm] * 8,
        out_specs=(vm, vm, vm, vm),
        scratch_shapes=[
            V(fd_modes.shape, f32),
            V((2, 64, 128), f32),
            V((6, 1, 128), jnp.int32),
            V(fsai_cols.shape, jnp.int32),
            V((T * 64, 128), f32),
            V((T * 64, 128), f32),
            V((64, T * 128), f32),
            V(((T + 2) * 64, 128), f32),
            V((64, T * 128), f32),
            V(fsai_blocks.shape, f32),
            V((128, T * 128), bf16),
            V((4, 64, 192), bf16),
            V((2, 256, 256), bf16),
            V((n, 8, 128), f32),
            V((8, 128), f32),
            V((n, 8, 128), f32),
            V((n, 8, 128), f32),
            V((2, 2, 32, 128), f32),
            V((2, 2, 32, 128), f32),
            V((2, 2, 32, 128), f32),
            V((2, 2, 32, 128), f32),
            V((8, 128), f32),
            V((n, 8, 128), f32),
            V(((T + 2) * 64, 128), f32),
            V((512, 128), f32),
            dma((8,)),
            dma, dma, dma, dma((2, 4)), dma,
        ],
        compiler_params=pltpu.CompilerParams(collective_id=0, has_side_effects=True,
                                             vmem_limit_bytes=48 * 1024 * 1024),
        cost_estimate=pl.CostEstimate(flops=10**9, bytes_accessed=8 * 2**20, transcendentals=0),
        name="step",
    )(*(pltpu.with_memory_space_constraint(v, pltpu.HBM) for v in (
        source, fd_modes, jnp.swapaxes(face_modes, 1, 2), coarse_map.reshape(-1, 1, coarse_map.shape[-1]),
        fsai_cols, capacity, fd_weights, fsai_blocks)))
    return pl.pallas_call(
        finish,
        out_shape=(field, field),
        in_specs=[vm] * 4,
        out_specs=(hbm, hbm),
        scratch_shapes=[V(source.shape, f32), V(source.shape, f32), dma((2,))],
        cost_estimate=pl.CostEstimate(flops=2**20, bytes_accessed=2 * 2**20, transcendentals=0),
        name="finish",
    )(*(pltpu.with_memory_space_constraint(v, pltpu.VMEM) for v in (p, img, x, alpha)))


def solution(mesh):
    in_specs = (
        P("sub", "cgrp"),
        P("sub", "cgrp"),
        P("sub", "cgrp"),
        P(),
        P(),
        P("sub", "cgrp", None, None),
        P(("sub", "cgrp"), None),
        P(("sub", "cgrp"), None, None, None),
    )
    out_specs = (P("sub", "cgrp"), P("sub", "cgrp"))
    step = functools.partial(body, mesh.shape["sub"], mesh.shape["cgrp"])
    return jax.shard_map(step, mesh=mesh, in_specs=in_specs, out_specs=out_specs, check_vma=False)
```
